32 devices in a mesh: pass: 8 (over z, y), blk: 4 (over x, core).
Axes of the slice: x: 2, y: 2, z: 4, core: 2. Of those that a mesh axis runs over, the one named last changes fastest.
Arguments:
- state: float32 [5, 32, 64, 1024], P(None, None, 'blk', 'pass'), as said below
- partner: int32 [8], replicated, may hold values from 0 to 7, as said below
- stencil: int32 [1024], P('pass'), may hold values from 0 to 15
- weight_table: float32 [16], replicated, may hold values from 0 to 1
Outputs:
- next_state: float32 [5, 32, 64, 1024], P(None, None, 'blk', 'pass')
The draws below stay inside these ranges and needn't reach their ends.
Inputs may be any that keep to these rules, and one draw needn't show every extreme that they name: partner[p] = (p + R) mod 8 for one R of 1 to 7 drawn for each step. `state`: every cell's density lies between 0.6 and 1.6 and its pressure between 0.4 and 1.2.
All inputs are finite; a program needn't handle non-finite values.
Results may differ from the reference program's by a relative error of at most 0.0003.
Values sent between devices are 32-bit elements; how exact they have to be, the bound alone decides.
A program may use at most 64 MiB of HBM per device.

```python
import jax
import jax.numpy as jnp
from jax import lax

CR = 32
CT = 128
NW = 16
PASSAGES = 8
CIRC = 1024
AX = 64


def draw_state(key, part):
    keys = jax.random.split(jax.random.fold_in(key, 11), 5)
    shape = (CR, AX, CIRC)
    rough = [jax.random.uniform(keys[i], shape, jnp.float32, -1.0, 1.0) for i in range(5)]
    density = jnp.exp(0.35 * rough[0])
    axial_velocity = 0.5 + 0.4 * rough[1]
    radial_velocity = 0.2 * rough[2]
    around_velocity = 0.6 * rough[3]
    pressure = 0.72 * jnp.exp(0.38 * rough[4])
    energy = pressure / 0.4 + 0.5 * density * (axial_velocity * axial_velocity + radial_velocity * radial_velocity + around_velocity * around_velocity)
    return jnp.stack([density, density * axial_velocity, density * radial_velocity, density * around_velocity, energy]).astype(jnp.float32)


def draw_partner(key, part):
    rotation = jax.random.randint(jax.random.fold_in(key, 23), (), 1, PASSAGES)
    return ((jnp.arange(PASSAGES, dtype=jnp.int32) + rotation) % PASSAGES).astype(jnp.int32)


def touch_ends(values, own_key, least, largest):
    place = [jax.random.randint(jax.random.fold_in(own_key, axis), (), 0, length) for axis, length in enumerate(values.shape)]
    widest = values.shape.index(max(values.shape))
    next_to = place[:widest] + [(place[widest] + 1) % values.shape[widest]] + place[widest + 1:]
    return values.at[tuple(place)].set(least).at[tuple(next_to)].set(largest)


def setup_inputs(seed: int = 0) -> dict:
    splits = jax.random.split(jax.random.key(seed), 5)
    state = draw_state(jax.random.fold_in(splits[4], 71), 0)
    partner = draw_partner(jax.random.fold_in(splits[4], 71), 0)
    stencil = touch_ends(jax.random.randint(splits[2], (CIRC,), 0, NW), jax.random.fold_in(splits[2], 1), 0, NW - 1).astype(jnp.int32)
    weight_table = jnp.clip(jax.random.uniform(splits[3], (NW,), jnp.float32, 0.0, 1.0), 0.0, 1.0)
    return {"state": state, "partner": partner, "stencil": stencil, "weight_table": weight_table}


GAMMA_MINUS = 0.4
GAMMA_VALUE = 1.4
AXIAL_COEF = 0.4
RADIAL_COEF = 0.3
AROUND_COEF = 0.3

def cell_parts(cells, component):
    density = cells[0]
    velocity = cells[component] / density
    pressure = GAMMA_MINUS * (cells[4] - 0.5 * (cells[1] * cells[1] + cells[2] * cells[2] + cells[3] * cells[3]) / density)
    sound_speed = jnp.sqrt(GAMMA_VALUE * pressure / density)
    flux = cells * velocity[None]
    flux = flux.at[component].add(pressure)
    flux = flux.at[4].add(pressure * velocity)
    return (flux, jnp.abs(velocity) + sound_speed)

def face_flux(left, right, component):
    flux_left, reach_left = cell_parts(left, component)
    flux_right, reach_right = cell_parts(right, component)
    return 0.5 * (flux_left + flux_right) - 0.5 * jnp.maximum(reach_left, reach_right)[None] * (right - left)

def residual_section(slab, ghost_rotor, ghost_stator, half_point):
    core = slab[:, 1:-1]
    rotor_cells = jnp.concatenate([core[:, :, :1], core[:, :, :half_point], ghost_rotor[:, :, None]], axis=2)
    stator_cells = jnp.concatenate([ghost_stator[:, :, None], core[:, :, half_point:], core[:, :, -1:]], axis=2)
    rotor_faces = face_flux(rotor_cells[:, :, :-1], rotor_cells[:, :, 1:], 1)
    stator_faces = face_flux(stator_cells[:, :, :-1], stator_cells[:, :, 1:], 1)
    axial_diff = jnp.concatenate([rotor_faces[:, :, 1:] - rotor_faces[:, :, :-1], stator_faces[:, :, 1:] - stator_faces[:, :, :-1]], axis=2)
    radial_faces = face_flux(slab[:, :-1], slab[:, 1:], 2)
    radial_diff = radial_faces[:, 1:] - radial_faces[:, :-1]
    beside_all = jnp.concatenate([core[..., -1:], core, core[..., :1]], axis=3)
    around_faces = face_flux(beside_all[..., :-1], beside_all[..., 1:], 3)
    around_diff = around_faces[..., 1:] - around_faces[..., :-1]
    return core - AXIAL_COEF * axial_diff - RADIAL_COEF * radial_diff - AROUND_COEF * around_diff

def reference(state, partner, stencil, weight_table):
    half_point = AX // 2
    shift = (partner[0] % PASSAGES).astype(jnp.int32) * CT
    weights = weight_table[stencil]
    stator_plane = state[:, :, half_point]
    rotor_plane = state[:, :, half_point - 1]
    ghost_rotor = weights * jnp.roll(stator_plane, -shift, axis=2) + (1.0 - weights) * jnp.roll(stator_plane, -shift - 1, axis=2)
    ghost_stator = weights * jnp.roll(rotor_plane, shift, axis=2) + (1.0 - weights) * jnp.roll(rotor_plane, shift + 1, axis=2)
    padded = jnp.concatenate([state[:, :1], state, state[:, -1:]], axis=1)
    block_rows = 4

    def one_block(block_index):
        start = (block_index * block_rows).astype(jnp.int32)
        slab = lax.dynamic_slice_in_dim(padded, start, block_rows + 2, axis=1)
        rotor_part = lax.dynamic_slice_in_dim(ghost_rotor, start, block_rows, axis=1)
        stator_part = lax.dynamic_slice_in_dim(ghost_stator, start, block_rows, axis=1)
        return residual_section(slab, rotor_part, stator_part, half_point)
    stacked = lax.map(one_block, jnp.arange(CR // block_rows, dtype=jnp.int32))
    return jnp.moveaxis(stacked, 0, 1).reshape(5, CR, AX, CIRC)
```

```python
import functools

import jax
import jax.numpy as jnp
from jax import lax
from jax.experimental import pallas as pl
from jax.experimental.pallas import tpu as pltpu
from jax.sharding import PartitionSpec as P

AXIAL_COEF = 0.4
RADIAL_COEF = 0.3
AROUND_COEF = 0.3
MESH = pl.DeviceIdType.MESH


def basics(q):
    inv = 1.0 / q[0]
    pressure = 0.4 * (q[4] - 0.5 * (q[1] * q[1] + q[2] * q[2] + q[3] * q[3]) * inv)
    return inv, pressure, jnp.sqrt(1.4 * pressure * inv)


def flux_of(q, base, d):
    inv, pressure, sound = base
    u = q[d] * inv
    flux = [c * u for c in q]
    flux[d] = flux[d] + pressure
    flux[4] = flux[4] + pressure * u
    return flux, jnp.abs(u) + sound


def between(left, flux_left, reach_left, right, flux_right, reach_right, scale):
    reach = jnp.maximum(reach_left, reach_right) * (0.5 * scale)
    return [
        (0.5 * scale) * (fl + fr) - reach * (b - a)
        for a, fl, b, fr in zip(left, flux_left, right, flux_right)
    ]


def face(left, right, d, scale):
    fl, rl = flux_of(left, basics(left), d)
    fr, rr = flux_of(right, basics(right), d)
    return between(left, fl, rl, right, fr, rr, scale)


def shifted_diff(q, base, d, axis, keep, scale):
    length = q[0].shape[axis]
    up = lambda x: pltpu.roll(x, length - 1, axis)
    flux, reach = flux_of(q, base, d)
    above = between(q, flux, reach, [up(c) for c in q], [up(c) for c in flux], up(reach), scale)
    above = [jnp.where(keep, c, 0.0) for c in above]
    return [c - pltpu.roll(c, 1, axis) for c in above]


def kernel(
    count, state, partner, stencil, table, out,
    planes, mate_in, gathered, outer, packed, left_in, right_in,
    plane_send, plane_recv, side_send, side_recv,
):
    me = lax.axis_index("pass")
    blk = lax.axis_index("blk")
    odd = lax.rem(blk, 2)
    mate = blk + 1 - 2 * odd
    facing = 3 - blk
    ahead, behind = lax.rem(me + 1, count), lax.rem(me + count - 1, count)
    radial, axial, lanes = state.shape[1:]
    interface = jnp.logical_or(blk == 1, blk == 2)

    barrier = pltpu.get_barrier_semaphore()
    for device in ((ahead, blk), (behind, blk), (me, mate)):
        pl.semaphore_signal(barrier, inc=1, device_id=device, device_id_type=MESH)

    @pl.when(interface)
    def _():
        for j in range(count):
            pl.semaphore_signal(barrier, inc=1, device_id=(j, facing), device_id_type=MESH)

    for f in range(5):
        planes[0, f] = state[f, :, 0, :]
        planes[1, f] = state[f, :, axial - 1, :]

    def plane_copy(k):
        target = lax.rem(me + k, count)
        return pltpu.make_async_remote_copy(
            src_ref=planes.at[odd], dst_ref=gathered.at[me],
            send_sem=plane_send.at[k], recv_sem=plane_recv.at[me],
            device_id=(target, facing), device_id_type=MESH,
        )

    def side_copy(k, src, dst, device):
        return pltpu.make_async_remote_copy(
            src_ref=src, dst_ref=dst, send_sem=side_send.at[k], recv_sem=side_recv.at[k],
            device_id=device, device_id_type=MESH,
        )

    @pl.when(interface)
    def _():
        pl.semaphore_wait(barrier, 3 + count)
        for k in range(count):
            plane_copy(k).start()

    @pl.when(jnp.logical_not(interface))
    def _():
        pl.semaphore_wait(barrier, 3)

    to_mate = side_copy(0, planes.at[1 - odd], mate_in, (me, mate))
    to_ahead = side_copy(1, packed, left_in, (ahead, blk))
    to_behind = side_copy(2, packed, right_in, (behind, blk))
    to_mate.start()

    lane = lax.broadcasted_iota(jnp.int32, (axial, lanes), 1)
    row = lax.broadcasted_iota(jnp.int32, (axial, lanes), 0)

    def pack(r, held):
        place = jnp.logical_or(lane == 2 * r, lane == lax.rem(2 * r - 1 + lanes, lanes))
        return tuple(
            jnp.where(place, pltpu.roll(state[f, r], 2 * r, 1), held[f]) for f in range(5)
        )

    held = lax.fori_loop(
        0, radial, pack, tuple(jnp.ones((axial, lanes), jnp.float32) for _ in range(5)), unroll=4
    )
    for f in range(5):
        packed[f] = held[f]
    to_ahead.start()
    to_behind.start()

    not_last_row = row < axial - 1
    not_last_lane = lane < lanes - 1

    def cells(r):
        return tuple(state[f, r] for f in range(5))

    def step(r, carry):
        q, base, flux, reach, below = carry
        following = cells(jnp.minimum(r + 1, radial - 1))
        base_f = basics(following)
        flux_f, reach_f = flux_of(following, base_f, 2)
        above = between(q, flux, reach, following, flux_f, reach_f, RADIAL_COEF)
        total = [c - (a - b) for c, a, b in zip(q, above, below)]
        part = shifted_diff(q, base, 1, 0, not_last_row, AXIAL_COEF)
        total = [c - a for c, a in zip(total, part)]
        part = shifted_diff(q, base, 3, 1, not_last_lane, AROUND_COEF)
        for f in range(5):
            out[f, r] = total[f] - part[f]
        return following, base_f, tuple(flux_f), reach_f, tuple(above)

    q0 = cells(0)
    base0 = basics(q0)
    flux0, reach0 = flux_of(q0, base0, 2)
    first = between(q0, flux0, reach0, q0, flux0, reach0, RADIAL_COEF)
    lax.fori_loop(0, radial, step, (q0, base0, tuple(flux0), reach0, tuple(first)))

    to_ahead.wait()
    to_behind.wait()
    even_lane = lax.rem(lane, 2) == 0
    left = [jnp.where(even_lane, pltpu.roll(left_in[f], 1, 1), packed[f]) for f in range(5)]
    right = [jnp.where(even_lane, packed[f], pltpu.roll(right_in[f], lanes - 1, 1)) for f in range(5)]
    sides = [jnp.where(even_lane, c, -c) for c in face(left, right, 3, AROUND_COEF)]
    ends = jnp.logical_or(lane == 0, lane == lanes - 1)

    def add_sides(r, _):
        for f in range(5):
            moved = pltpu.roll(sides[f], lax.rem(lanes - 2 * r, lanes), 1)
            out[f, r] = out[f, r] + jnp.where(ends, moved, 0.0)
        return 0

    lax.fori_loop(0, radial, add_sides, 0, unroll=2)

    to_mate.wait()

    @pl.when(jnp.logical_not(interface))
    def _():
        outer[...] = planes[odd]

    @pl.when(interface)
    def _():
        for k in range(count):
            pltpu.make_async_remote_copy(
                src_ref=planes.at[odd], dst_ref=gathered.at[k],
                send_sem=plane_send.at[k], recv_sem=plane_recv.at[k],
                device_id=(k, facing), device_id_type=MESH,
            ).wait()
        weights = jnp.zeros((1, lanes), jnp.float32)
        for k in range(table.shape[0]):
            weights = jnp.where(stencil[...] == k, table[k], weights)
        offset = lax.rem(partner[me] - me + count, count)
        plane_lane = lax.broadcasted_iota(jnp.int32, (radial, lanes), 1)

        def ghost(main_at, edge_at, shift, edge_lane):
            for f in range(5):
                main = gathered[main_at, f]
                edge = gathered[edge_at, f]
                beside = jnp.where(
                    plane_lane == edge_lane, pltpu.roll(edge, shift, 1), pltpu.roll(main, shift, 1)
                )
                outer[f] = weights * main + (1.0 - weights) * beside

        @pl.when(blk == 1)
        def _():
            at = lax.rem(me + offset, count)
            ghost(at, lax.rem(at + 1, count), lanes - 1, lanes - 1)

        @pl.when(blk == 2)
        def _():
            at = lax.rem(me - offset + count, count)
            ghost(at, lax.rem(at + count - 1, count), 1, 0)

    def add_lower(beside):
        for start in range(0, radial, 8):
            rows = slice(start, start + 8)
            flux = face(
                [beside[f, rows] for f in range(5)], [planes[0, f, rows] for f in range(5)], 1, AXIAL_COEF
            )
            for f in range(5):
                out[f, rows, 0, :] = out[f, rows, 0, :] + flux[f]

    def add_upper(beside):
        for start in range(0, radial, 8):
            rows = slice(start, start + 8)
            flux = face(
                [planes[1, f, rows] for f in range(5)], [beside[f, rows] for f in range(5)], 1, AXIAL_COEF
            )
            for f in range(5):
                out[f, rows, axial - 1, :] = out[f, rows, axial - 1, :] - flux[f]

    @pl.when(odd == 0)
    def _():
        add_lower(outer)
        add_upper(mate_in)

    @pl.when(odd == 1)
    def _():
        add_lower(mate_in)
        add_upper(outer)


def shards(state, partner, stencil, weight_table):
    count = lax.axis_size("pass")
    _, radial, axial, lanes = state.shape
    vmem = pl.BlockSpec(memory_space=pltpu.VMEM)
    smem = pl.BlockSpec(memory_space=pltpu.SMEM)
    f32 = jnp.float32
    return pl.pallas_call(
        functools.partial(kernel, count),
        out_shape=jax.ShapeDtypeStruct(state.shape, f32),
        in_specs=[vmem, smem, vmem, smem],
        out_specs=vmem,
        scratch_shapes=[
            pltpu.VMEM((2, 5, radial, lanes), f32),
            pltpu.VMEM((5, radial, lanes), f32),
            pltpu.VMEM((count, 5, radial, lanes), f32),
            pltpu.VMEM((5, radial, lanes), f32),
            pltpu.VMEM((5, axial, lanes), f32),
            pltpu.VMEM((5, axial, lanes), f32),
            pltpu.VMEM((5, axial, lanes), f32),
            pltpu.SemaphoreType.DMA((count,)),
            pltpu.SemaphoreType.DMA((count,)),
            pltpu.SemaphoreType.DMA((3,)),
            pltpu.SemaphoreType.DMA((3,)),
        ],
        compiler_params=pltpu.CompilerParams(
            collective_id=0, has_side_effects=True, vmem_limit_bytes=24 * 1024 * 1024
        ),
        cost_estimate=pl.CostEstimate(
            flops=200 * radial * axial * lanes, bytes_accessed=8 * state.size, transcendentals=0
        ),
    )(state, partner, stencil.reshape(1, lanes), weight_table)


def solution(mesh):
    placed = (P(None, None, "blk", "pass"), P(), P("pass"), P())
    return jax.shard_map(
        shards, mesh=mesh, in_specs=placed, out_specs=P(None, None, "blk", "pass"), check_vma=False
    )
```

```python
import functools

import jax
import jax.numpy as jnp
from jax import lax
from jax.experimental import pallas as pl
from jax.experimental.pallas import tpu as pltpu
from jax.sharding import PartitionSpec as P

AXIAL_COEF = 0.4
RADIAL_COEF = 0.3
AROUND_COEF = 0.3
MESH = pl.DeviceIdType.MESH


def basics(q):
    inv = 1.0 / q[0]
    pressure = 0.4 * (q[4] - 0.5 * (q[1] * q[1] + q[2] * q[2] + q[3] * q[3]) * inv)
    square = 1.4 * pressure * inv
    return inv, pressure, square * lax.rsqrt(square)


def flux_of(q, base, d):
    inv, pressure, sound = base
    u = q[d] * inv
    flux = [c * u for c in q]
    flux[d] = flux[d] + pressure
    flux[4] = flux[4] + pressure * u
    return flux, jnp.abs(u) + sound


def between(left, flux_left, reach_left, right, flux_right, reach_right, scale):
    reach = jnp.maximum(reach_left, reach_right) * (0.5 * scale)
    return [
        (0.5 * scale) * (fl + fr) - reach * (b - a)
        for a, fl, b, fr in zip(left, flux_left, right, flux_right)
    ]


def face(left, right, d, scale):
    fl, rl = flux_of(left, basics(left), d)
    fr, rr = flux_of(right, basics(right), d)
    return between(left, fl, rl, right, fr, rr, scale)


def shifted_diff(q, base, d, axis, keep, scale):
    length = q[0].shape[axis]
    up = lambda x: pltpu.roll(x, length - 1, axis)
    flux, reach = flux_of(q, base, d)
    above = between(q, flux, reach, [up(c) for c in q], [up(c) for c in flux], up(reach), scale)
    above = [jnp.where(keep, c, 0.0) for c in above]
    return [c - pltpu.roll(c, 1, axis) for c in above]


def kernel(
    count, turn, state_in, partner_in, stencil_in, table_in, out,
    state, partner, stencil, table,
    planes, mate_in, gathered, edge_out, edge_in, outer, packed, left_in, right_in,
    plane_send, plane_recv, side_send, side_recv, load_sem,
):
    me = lax.axis_index("pass")
    blk = lax.axis_index("blk")
    odd = lax.rem(blk, 2)
    mate = blk + 1 - 2 * odd
    facing = 3 - blk
    ahead, behind = lax.rem(me + 1, count), lax.rem(me + count - 1, count)
    radial, axial, lanes = state.shape[1:]
    interface = jnp.logical_or(blk == 1, blk == 2)
    if turn is None:
        partners = list(range(count))
    else:
        sign = jnp.where(blk == 1, 1, -1)
        partners = [lax.rem(me + sign * (turn + k) + 2 * count, count) for k in range(2)]

    loads = [pltpu.make_async_copy(state_in, state, load_sem.at[0])]
    loads.append(pltpu.make_async_copy(stencil_in, stencil, load_sem.at[1]))
    loads.append(pltpu.make_async_copy(table_in, table, load_sem.at[2]))
    if turn is None:
        loads.append(pltpu.make_async_copy(partner_in, partner, load_sem.at[3]))
    for load in loads:
        load.start()

    barrier = pltpu.get_barrier_semaphore()
    for device in ((ahead, blk), (behind, blk), (me, mate)):
        pl.semaphore_signal(barrier, inc=1, device_id=device, device_id_type=MESH)

    @pl.when(interface)
    def _():
        for j in partners:
            pl.semaphore_signal(barrier, inc=1, device_id=(j, facing), device_id_type=MESH)

    loads[0].wait()
    for f in range(5):
        planes[0, f] = state[f, :, 0, :]
        planes[1, f] = state[f, :, axial - 1, :]
    plane_lane = lax.broadcasted_iota(jnp.int32, (radial, lanes), 1)

    def plane_copies():
        if turn is None:
            return [
                pltpu.make_async_remote_copy(
                    src_ref=planes.at[odd], dst_ref=gathered.at[me],
                    send_sem=plane_send.at[j], recv_sem=plane_recv.at[me],
                    device_id=(j, facing), device_id_type=MESH,
                )
                for j in partners
            ]
        return [
            pltpu.make_async_remote_copy(
                src_ref=src, dst_ref=dst, send_sem=plane_send.at[k], recv_sem=plane_recv.at[k],
                device_id=(partners[k], facing), device_id_type=MESH,
            )
            for k, (src, dst) in enumerate(
                ((planes.at[odd], gathered.at[0]), (edge_out, edge_in))
            )
        ]

    def side_copy(k, src, dst, device):
        return pltpu.make_async_remote_copy(
            src_ref=src, dst_ref=dst, send_sem=side_send.at[k], recv_sem=side_recv.at[k],
            device_id=device, device_id_type=MESH,
        )

    @pl.when(interface)
    def _():
        if turn is not None:
            edge = jnp.zeros((radial, lanes), jnp.float32)
            for f in range(5):
                first = pltpu.roll(planes[0, f], f, 1)
                last = pltpu.roll(planes[1, f], f + 1, 1)
                edge = jnp.where(plane_lane == f, jnp.where(blk == 1, last, first), edge)
            edge_out[...] = edge
        pl.semaphore_wait(barrier, 3 + len(partners))
        for copy in plane_copies():
            copy.start()

    @pl.when(jnp.logical_not(interface))
    def _():
        pl.semaphore_wait(barrier, 3)

    to_mate = side_copy(0, planes.at[1 - odd], mate_in, (me, mate))
    to_ahead = side_copy(1, packed, left_in, (ahead, blk))
    to_behind = side_copy(2, packed, right_in, (behind, blk))
    to_mate.start()

    lane = lax.broadcasted_iota(jnp.int32, (axial, lanes), 1)
    row = lax.broadcasted_iota(jnp.int32, (axial, lanes), 0)

    def pack(r, held):
        place = jnp.logical_or(lane == 2 * r, lane == lax.rem(2 * r - 1 + lanes, lanes))
        return tuple(
            jnp.where(place, pltpu.roll(state[f, r], 2 * r, 1), held[f]) for f in range(5)
        )

    held = lax.fori_loop(
        0, radial, pack, tuple(jnp.ones((axial, lanes), jnp.float32) for _ in range(5)), unroll=8
    )
    for f in range(5):
        packed[f] = held[f]
    to_ahead.start()
    to_behind.start()

    not_last_row = row < axial - 1
    not_last_lane = lane < lanes - 1

    def cells(r):
        return tuple(state[f, r] for f in range(5))

    def step(r, carry):
        q, base, flux, reach, below = carry
        following = cells(jnp.minimum(r + 1, radial - 1))
        base_f = basics(following)
        flux_f, reach_f = flux_of(following, base_f, 2)
        above = between(q, flux, reach, following, flux_f, reach_f, RADIAL_COEF)
        total = [c - (a - b) for c, a, b in zip(q, above, below)]
        part = shifted_diff(q, base, 1, 0, not_last_row, AXIAL_COEF)
        total = [c - a for c, a in zip(total, part)]
        part = shifted_diff(q, base, 3, 1, not_last_lane, AROUND_COEF)
        for f in range(5):
            out[f, r] = total[f] - part[f]
        return following, base_f, tuple(flux_f), reach_f, tuple(above)

    q0 = cells(0)
    base0 = basics(q0)
    flux0, reach0 = flux_of(q0, base0, 2)
    first = between(q0, flux0, reach0, q0, flux0, reach0, RADIAL_COEF)
    lax.fori_loop(0, radial, step, (q0, base0, tuple(flux0), reach0, tuple(first)), unroll=4)

    to_ahead.wait()
    to_behind.wait()
    even_lane = lax.rem(lane, 2) == 0
    left = [jnp.where(even_lane, pltpu.roll(left_in[f], 1, 1), packed[f]) for f in range(5)]
    right = [jnp.where(even_lane, packed[f], pltpu.roll(right_in[f], lanes - 1, 1)) for f in range(5)]
    sides = [jnp.where(even_lane, c, -c) for c in face(left, right, 3, AROUND_COEF)]
    ends = jnp.logical_or(lane == 0, lane == lanes - 1)

    def add_sides(r, _):
        for f in range(5):
            moved = pltpu.roll(sides[f], lax.rem(lanes - 2 * r, lanes), 1)
            out[f, r] = out[f, r] + jnp.where(ends, moved, 0.0)
        return 0

    lax.fori_loop(0, radial, add_sides, 0, unroll=8)

    to_mate.wait()
    for load in loads[1:]:
        load.wait()

    @pl.when(jnp.logical_not(interface))
    def _():
        outer[...] = planes[odd]

    @pl.when(interface)
    def _():
        if turn is None:
            for k in range(count):
                pltpu.make_async_remote_copy(
                    src_ref=planes.at[odd], dst_ref=gathered.at[k],
                    send_sem=plane_send.at[k], recv_sem=plane_recv.at[k],
                    device_id=(k, facing), device_id_type=MESH,
                ).wait()
        else:
            for copy in plane_copies():
                copy.wait()
        weights = jnp.zeros((1, lanes), jnp.float32)
        for k in range(table.shape[0]):
            weights = jnp.where(stencil[...] == k, table[k], weights)
        offset = 0 if turn is not None else lax.rem(partner[me] - me + count, count)

        def ghost(main_at, edge_at, shift, edge_lane):
            for f in range(5):
                main = gathered[0, f] if turn is not None else gathered[main_at, f]
                if turn is not None:
                    edge = pltpu.roll(edge_in[...], (edge_lane - f) % lanes, 1)
                else:
                    edge = pltpu.roll(gathered[edge_at, f], shift, 1)
                beside = jnp.where(plane_lane == edge_lane, edge, pltpu.roll(main, shift, 1))
                outer[f] = weights * main + (1.0 - weights) * beside

        @pl.when(blk == 1)
        def _():
            at = lax.rem(me + offset, count)
            ghost(at, lax.rem(at + 1, count), lanes - 1, lanes - 1)

        @pl.when(blk == 2)
        def _():
            at = lax.rem(me - offset + count, count)
            ghost(at, lax.rem(at + count - 1, count), 1, 0)

    def add_lower(beside):
        for start in range(0, radial, 8):
            rows = slice(start, start + 8)
            flux = face(
                [beside[f, rows] for f in range(5)], [planes[0, f, rows] for f in range(5)], 1, AXIAL_COEF
            )
            for f in range(5):
                out[f, rows, 0, :] = out[f, rows, 0, :] + flux[f]

    def add_upper(beside):
        for start in range(0, radial, 8):
            rows = slice(start, start + 8)
            flux = face(
                [planes[1, f, rows] for f in range(5)], [beside[f, rows] for f in range(5)], 1, AXIAL_COEF
            )
            for f in range(5):
                out[f, rows, axial - 1, :] = out[f, rows, axial - 1, :] - flux[f]

    @pl.when(odd == 0)
    def _():
        add_lower(outer)
        add_upper(mate_in)

    @pl.when(odd == 1)
    def _():
        add_lower(mate_in)
        add_upper(outer)


def section(turn, state, partner, stencil, weight_table):
    count = lax.axis_size("pass")
    _, radial, axial, lanes = state.shape
    hbm = pl.BlockSpec(memory_space=pltpu.HBM)
    f32 = jnp.float32
    held = count if turn is None else 1
    copies = count if turn is None else 2
    return pl.pallas_call(
        functools.partial(kernel, count, turn),
        out_shape=jax.ShapeDtypeStruct(state.shape, f32),
        in_specs=[hbm] * 4,
        out_specs=pl.BlockSpec(memory_space=pltpu.VMEM),
        scratch_shapes=[
            pltpu.VMEM(state.shape, f32),
            pltpu.SMEM(partner.shape, jnp.int32),
            pltpu.VMEM(stencil.shape, jnp.int32),
            pltpu.SMEM(weight_table.shape, f32),
            pltpu.VMEM((2, 5, radial, lanes), f32),
            pltpu.VMEM((5, radial, lanes), f32),
            pltpu.VMEM((held, 5, radial, lanes), f32),
            pltpu.VMEM((radial, lanes), f32),
            pltpu.VMEM((radial, lanes), f32),
            pltpu.VMEM((5, radial, lanes), f32),
            pltpu.VMEM((5, axial, lanes), f32),
            pltpu.VMEM((5, axial, lanes), f32),
            pltpu.VMEM((5, axial, lanes), f32),
            pltpu.SemaphoreType.DMA((copies,)),
            pltpu.SemaphoreType.DMA((copies,)),
            pltpu.SemaphoreType.DMA((3,)),
            pltpu.SemaphoreType.DMA((3,)),
            pltpu.SemaphoreType.DMA((4,)),
        ],
        compiler_params=pltpu.CompilerParams(
            collective_id=turn or 0, has_side_effects=True, vmem_limit_bytes=24 * 1024 * 1024
        ),
        cost_estimate=pl.CostEstimate(
            flops=200 * radial * axial * lanes, bytes_accessed=8 * state.size, transcendentals=0
        ),
    )(state, partner, stencil, weight_table)


def shards(state, partner, stencil, weight_table):
    count = lax.axis_size("pass")
    operands = (state, partner, stencil.reshape(1, -1), weight_table)
    if count > 8:
        return section(None, *operands)
    return lax.switch(
        partner[0] - 1, [functools.partial(section, k) for k in range(1, count)], *operands
    )


def solution(mesh):
    placed = (P(None, None, "blk", "pass"), P(), P("pass"), P())
    return jax.shard_map(
        shards, mesh=mesh, in_specs=placed, out_specs=P(None, None, "blk", "pass"), check_vma=False
    )
```

```python
import functools

import jax
import jax.numpy as jnp
from jax import lax
from jax.experimental import pallas as pl
from jax.experimental.pallas import tpu as pltpu
from jax.sharding import PartitionSpec as P

AXIAL_COEF = 0.4
RADIAL_COEF = 0.3
AROUND_COEF = 0.3
MESH = pl.DeviceIdType.MESH


def basics(q):
    inv = 1.0 / q[0]
    pressure = 0.4 * (q[4] - 0.5 * (q[1] * q[1] + q[2] * q[2] + q[3] * q[3]) * inv)
    square = 1.4 * pressure * inv
    return inv, pressure, square * lax.rsqrt(square)


def flux_of(q, base, d, scale):
    inv, pressure, sound = base
    u = q[d] * (inv * (0.5 * scale))
    part = pressure * (0.5 * scale)
    flux = [c * u for c in q]
    flux[d] = flux[d] + part
    flux[4] = flux[4] + pressure * u
    return flux, jnp.abs(u) + sound * (0.5 * scale)


def between(left, flux_left, reach_left, right, flux_right, reach_right):
    reach = jnp.maximum(reach_left, reach_right)
    return [
        (fl + fr) - reach * (b - a)
        for a, fl, b, fr in zip(left, flux_left, right, flux_right)
    ]


def face(left, right, d, scale):
    fl, rl = flux_of(left, basics(left), d, scale)
    fr, rr = flux_of(right, basics(right), d, scale)
    return between(left, fl, rl, right, fr, rr)


def shifted_diff(q, base, d, axis, keep, scale):
    length = q[0].shape[axis]
    up = lambda x: pltpu.roll(x, length - 1, axis)
    flux, reach = flux_of(q, base, d, scale)
    above = between(q, flux, reach, [up(c) for c in q], [up(c) for c in flux], up(reach))
    above = [jnp.where(keep, c, 0.0) for c in above]
    return [c - pltpu.roll(c, 1, axis) for c in above]


def kernel(
    count, turn, state_in, partner_in, stencil_in, table_in, out,
    state, partner, stencil, table,
    planes, mate_in, gathered, edge_out, edge_in, outer, packed, left_in, right_in,
    plane_send, plane_recv, side_send, side_recv, load_sem,
):
    me = lax.axis_index("pass")
    blk = lax.axis_index("blk")
    odd = lax.rem(blk, 2)
    mate = blk + 1 - 2 * odd
    facing = 3 - blk
    ahead, behind = lax.rem(me + 1, count), lax.rem(me + count - 1, count)
    radial, axial, lanes = state.shape[1:]
    interface = jnp.logical_or(blk == 1, blk == 2)
    if turn is None:
        partners = list(range(count))
    else:
        sign = jnp.where(blk == 1, 1, -1)
        partners = [lax.rem(me + sign * (turn + k) + 2 * count, count) for k in range(2)]

    loads = [pltpu.make_async_copy(state_in, state, load_sem.at[0])]
    loads.append(pltpu.make_async_copy(stencil_in, stencil, load_sem.at[1]))
    loads.append(pltpu.make_async_copy(table_in, table, load_sem.at[2]))
    if turn is None:
        loads.append(pltpu.make_async_copy(partner_in, partner, load_sem.at[3]))
    for load in loads:
        load.start()

    barrier = pltpu.get_barrier_semaphore()
    for device in ((ahead, blk), (behind, blk), (me, mate)):
        pl.semaphore_signal(barrier, inc=1, device_id=device, device_id_type=MESH)

    @pl.when(interface)
    def _():
        for j in partners:
            pl.semaphore_signal(barrier, inc=1, device_id=(j, facing), device_id_type=MESH)

    loads[0].wait()
    for f in range(5):
        planes[0, f] = state[f, :, 0, :]
        planes[1, f] = state[f, :, axial - 1, :]
    plane_lane = lax.broadcasted_iota(jnp.int32, (radial, lanes), 1)

    def plane_copies():
        if turn is None:
            return [
                pltpu.make_async_remote_copy(
                    src_ref=planes.at[odd], dst_ref=gathered.at[me],
                    send_sem=plane_send.at[j], recv_sem=plane_recv.at[me],
                    device_id=(j, facing), device_id_type=MESH,
                )
                for j in partners
            ]
        return [
            pltpu.make_async_remote_copy(
                src_ref=src, dst_ref=dst, send_sem=plane_send.at[k], recv_sem=plane_recv.at[k],
                device_id=(partners[k], facing), device_id_type=MESH,
            )
            for k, (src, dst) in enumerate(
                ((planes.at[odd], gathered.at[0]), (edge_out, edge_in))
            )
        ]

    def side_copy(k, src, dst, device):
        return pltpu.make_async_remote_copy(
            src_ref=src, dst_ref=dst, send_sem=side_send.at[k], recv_sem=side_recv.at[k],
            device_id=device, device_id_type=MESH,
        )

    lane = lax.broadcasted_iota(jnp.int32, (axial, lanes), 1)
    row = lax.broadcasted_iota(jnp.int32, (axial, lanes), 0)

    def pack(r, held):
        place = jnp.logical_or(lane == 2 * r, lane == lax.rem(2 * r - 1 + lanes, lanes))
        return tuple(
            jnp.where(place, pltpu.roll(state[f, r], 2 * r, 1), held[f]) for f in range(5)
        )

    held = lax.fori_loop(
        0, radial, pack, tuple(jnp.ones((axial, lanes), jnp.float32) for _ in range(5)), unroll=8
    )
    for f in range(5):
        packed[f] = held[f]

    if turn is not None:

        @pl.when(interface)
        def _():
            edge = jnp.zeros((radial, lanes), jnp.float32)
            for f in range(5):
                first = pltpu.roll(planes[0, f], f, 1)
                last = pltpu.roll(planes[1, f], f + 1, 1)
                edge = jnp.where(plane_lane == f, jnp.where(blk == 1, last, first), edge)
            edge_out[...] = edge

    not_last_row = row < axial - 1
    not_last_lane = lane < lanes - 1

    def cells(r):
        return tuple(state[f, r] for f in range(5))

    def step(r, carry):
        q, base, flux, reach, below = carry
        following = cells(jnp.minimum(r + 1, radial - 1))
        base_f = basics(following)
        flux_f, reach_f = flux_of(following, base_f, 2, RADIAL_COEF)
        above = between(q, flux, reach, following, flux_f, reach_f)
        total = [c - (a - b) for c, a, b in zip(q, above, below)]
        part = shifted_diff(q, base, 1, 0, not_last_row, AXIAL_COEF)
        total = [c - a for c, a in zip(total, part)]
        part = shifted_diff(q, base, 3, 1, not_last_lane, AROUND_COEF)
        for f in range(5):
            out[f, r] = total[f] - part[f]
        return following, base_f, tuple(flux_f), reach_f, tuple(above)

    q0 = cells(0)
    base0 = basics(q0)
    flux0, reach0 = flux_of(q0, base0, 2, RADIAL_COEF)
    first = between(q0, flux0, reach0, q0, flux0, reach0)
    carry = (q0, base0, tuple(flux0), reach0, tuple(first))
    carry = lax.fori_loop(0, radial // 4, step, carry, unroll=4)

    @pl.when(interface)
    def _():
        pl.semaphore_wait(barrier, 3 + len(partners))
        for copy in plane_copies():
            copy.start()

    @pl.when(jnp.logical_not(interface))
    def _():
        pl.semaphore_wait(barrier, 3)

    to_mate = side_copy(0, planes.at[1 - odd], mate_in, (me, mate))
    to_ahead = side_copy(1, packed, left_in, (ahead, blk))
    to_behind = side_copy(2, packed, right_in, (behind, blk))
    to_mate.start()
    to_ahead.start()
    to_behind.start()

    lax.fori_loop(radial // 4, radial, step, carry, unroll=4)

    def add_lower(beside):
        for start in range(0, radial, 8):
            rows = slice(start, start + 8)
            flux = face(
                [beside[f, rows] for f in range(5)], [planes[0, f, rows] for f in range(5)], 1, AXIAL_COEF
            )
            for f in range(5):
                out[f, rows, 0, :] = out[f, rows, 0, :] + flux[f]

    def add_upper(beside):
        for start in range(0, radial, 8):
            rows = slice(start, start + 8)
            flux = face(
                [planes[1, f, rows] for f in range(5)], [beside[f, rows] for f in range(5)], 1, AXIAL_COEF
            )
            for f in range(5):
                out[f, rows, axial - 1, :] = out[f, rows, axial - 1, :] - flux[f]

    to_mate.wait()

    @pl.when(odd == 0)
    def _():
        add_upper(mate_in)

    @pl.when(odd == 1)
    def _():
        add_lower(mate_in)

    to_ahead.wait()
    to_behind.wait()
    even_lane = lax.rem(lane, 2) == 0
    left = [jnp.where(even_lane, pltpu.roll(left_in[f], 1, 1), packed[f]) for f in range(5)]
    right = [jnp.where(even_lane, packed[f], pltpu.roll(right_in[f], lanes - 1, 1)) for f in range(5)]
    sides = [jnp.where(even_lane, c, -c) for c in face(left, right, 3, AROUND_COEF)]
    ends = jnp.logical_or(lane == 0, lane == lanes - 1)

    def add_sides(r, _):
        for f in range(5):
            moved = pltpu.roll(sides[f], lax.rem(lanes - 2 * r, lanes), 1)
            out[f, r] = out[f, r] + jnp.where(ends, moved, 0.0)
        return 0

    lax.fori_loop(0, radial, add_sides, 0, unroll=8)

    for load in loads[1:]:
        load.wait()

    @pl.when(jnp.logical_not(interface))
    def _():
        outer[...] = planes[odd]

    @pl.when(interface)
    def _():
        if turn is None:
            for k in range(count):
                pltpu.make_async_remote_copy(
                    src_ref=planes.at[odd], dst_ref=gathered.at[k],
                    send_sem=plane_send.at[k], recv_sem=plane_recv.at[k],
                    device_id=(k, facing), device_id_type=MESH,
                ).wait()
        else:
            for copy in plane_copies():
                copy.wait()
        weights = jnp.zeros((1, lanes), jnp.float32)
        for k in range(table.shape[0]):
            weights = jnp.where(stencil[...] == k, table[k], weights)
        offset = 0 if turn is not None else lax.rem(partner[me] - me + count, count)

        def ghost(main_at, edge_at, shift, edge_lane):
            for f in range(5):
                main = gathered[0, f] if turn is not None else gathered[main_at, f]
                if turn is not None:
                    edge = pltpu.roll(edge_in[...], (edge_lane - f) % lanes, 1)
                else:
                    edge = pltpu.roll(gathered[edge_at, f], shift, 1)
                beside = jnp.where(plane_lane == edge_lane, edge, pltpu.roll(main, shift, 1))
                outer[f] = weights * main + (1.0 - weights) * beside

        @pl.when(blk == 1)
        def _():
            at = lax.rem(me + offset, count)
            ghost(at, lax.rem(at + 1, count), lanes - 1, lanes - 1)

        @pl.when(blk == 2)
        def _():
            at = lax.rem(me - offset + count, count)
            ghost(at, lax.rem(at + count - 1, count), 1, 0)

    @pl.when(odd == 0)
    def _():
        add_lower(outer)

    @pl.when(odd == 1)
    def _():
        add_upper(outer)


def section(turn, state, partner, stencil, weight_table):
    count = lax.axis_size("pass")
    _, radial, axial, lanes = state.shape
    hbm = pl.BlockSpec(memory_space=pltpu.HBM)
    f32 = jnp.float32
    held = count if turn is None else 1
    copies = count if turn is None else 2
    return pl.pallas_call(
        functools.partial(kernel, count, turn),
        out_shape=jax.ShapeDtypeStruct(state.shape, f32),
        in_specs=[hbm] * 4,
        out_specs=pl.BlockSpec(memory_space=pltpu.VMEM),
        scratch_shapes=[
            pltpu.VMEM(state.shape, f32),
            pltpu.SMEM(partner.shape, jnp.int32),
            pltpu.VMEM(stencil.shape, jnp.int32),
            pltpu.SMEM(weight_table.shape, f32),
            pltpu.VMEM((2, 5, radial, lanes), f32),
            pltpu.VMEM((5, radial, lanes), f32),
            pltpu.VMEM((held, 5, radial, lanes), f32),
            pltpu.VMEM((radial, lanes), f32),
            pltpu.VMEM((radial, lanes), f32),
            pltpu.VMEM((5, radial, lanes), f32),
            pltpu.VMEM((5, axial, lanes), f32),
            pltpu.VMEM((5, axial, lanes), f32),
            pltpu.VMEM((5, axial, lanes), f32),
            pltpu.SemaphoreType.DMA((copies,)),
            pltpu.SemaphoreType.DMA((copies,)),
            pltpu.SemaphoreType.DMA((3,)),
            pltpu.SemaphoreType.DMA((3,)),
            pltpu.SemaphoreType.DMA((4,)),
        ],
        compiler_params=pltpu.CompilerParams(
            collective_id=turn or 0, has_side_effects=True, vmem_limit_bytes=24 * 1024 * 1024
        ),
        cost_estimate=pl.CostEstimate(
            flops=200 * radial * axial * lanes, bytes_accessed=8 * state.size, transcendentals=0
        ),
    )(state, partner, stencil, weight_table)


def shards(state, partner, stencil, weight_table):
    count = lax.axis_size("pass")
    operands = (state, partner, stencil.reshape(1, -1), weight_table)
    if count > 8:
        return section(None, *operands)
    return lax.switch(
        partner[0] - 1, [functools.partial(section, k) for k in range(1, count)], *operands
    )


def solution(mesh):
    placed = (P(None, None, "blk", "pass"), P(), P("pass"), P())
    return jax.shard_map(
        shards, mesh=mesh, in_specs=placed, out_specs=P(None, None, "blk", "pass"), check_vma=False
    )
```

```python
import functools

import jax
import jax.numpy as jnp
from jax import lax
from jax.experimental import pallas as pl
from jax.experimental.pallas import tpu as pltpu
from jax.sharding import PartitionSpec as P

AXIAL_COEF = 0.4
RADIAL_COEF = 0.3
AROUND_COEF = 0.3
MESH = pl.DeviceIdType.MESH


def basics(q):
    inv = 1.0 / q[0]
    pressure = 0.4 * (q[4] - 0.5 * (q[1] * q[1] + q[2] * q[2] + q[3] * q[3]) * inv)
    square = 1.4 * pressure * inv
    return inv, pressure, square * lax.rsqrt(square)


def flux_of(q, base, d, scale):
    inv, pressure, sound = base
    u = q[d] * (inv * (0.5 * scale))
    part = pressure * (0.5 * scale)
    flux = [c * u for c in q]
    flux[d] = flux[d] + part
    flux[4] = flux[4] + pressure * u
    return flux, jnp.abs(u) + sound * (0.5 * scale)


def between(left, flux_left, reach_left, right, flux_right, reach_right):
    reach = jnp.maximum(reach_left, reach_right)
    return [
        (fl + fr) - reach * (b - a)
        for a, fl, b, fr in zip(left, flux_left, right, flux_right)
    ]


def face(left, right, d, scale):
    fl, rl = flux_of(left, basics(left), d, scale)
    fr, rr = flux_of(right, basics(right), d, scale)
    return between(left, fl, rl, right, fr, rr)


def shifted_diff(q, base, d, axis, keep, scale):
    length = q[0].shape[axis]
    up = lambda x: pltpu.roll(x, length - 1, axis)
    flux, reach = flux_of(q, base, d, scale)
    above = between(q, flux, reach, [up(c) for c in q], [up(c) for c in flux], up(reach))
    above = [jnp.where(keep, c, 0.0) for c in above]
    return [c - pltpu.roll(c, 1, axis) for c in above]


def kernel(
    count, turn, state_in, partner_in, stencil_in, table_in, out,
    state, partner, stencil, table,
    planes, mate_in, gathered, edge_out, edge_in, outer, firsts, lasts, left_in, right_in,
    plane_send, plane_recv, side_send, side_recv, load_sem,
):
    me = lax.axis_index("pass")
    blk = lax.axis_index("blk")
    odd = lax.rem(blk, 2)
    mate = blk + 1 - 2 * odd
    facing = 3 - blk
    ahead, behind = lax.rem(me + 1, count), lax.rem(me + count - 1, count)
    radial, axial, lanes = state.shape[1:]
    interface = jnp.logical_or(blk == 1, blk == 2)
    if turn is None:
        partners = list(range(count))
    else:
        sign = jnp.where(blk == 1, 1, -1)
        partners = [lax.rem(me + sign * (turn + k) + 2 * count, count) for k in range(2)]

    loads = [pltpu.make_async_copy(state_in.at[f], state.at[f], load_sem.at[f]) for f in range(5)]
    loads.append(pltpu.make_async_copy(stencil_in, stencil, load_sem.at[5]))
    loads.append(pltpu.make_async_copy(table_in, table, load_sem.at[6]))
    if turn is None:
        loads.append(pltpu.make_async_copy(partner_in, partner, load_sem.at[7]))
    for load in loads:
        load.start()

    barrier = pltpu.get_barrier_semaphore()
    for device in ((ahead, blk), (behind, blk), (me, mate)):
        pl.semaphore_signal(barrier, inc=1, device_id=device, device_id_type=MESH)

    @pl.when(interface)
    def _():
        for j in partners:
            pl.semaphore_signal(barrier, inc=1, device_id=(j, facing), device_id_type=MESH)

    for f in range(5):
        loads[f].wait()
        planes[0, f] = state[f, :, 0, :]
        planes[1, f] = state[f, :, axial - 1, :]
    plane_lane = lax.broadcasted_iota(jnp.int32, (radial, lanes), 1)

    def plane_copies():
        if turn is None:
            return [
                pltpu.make_async_remote_copy(
                    src_ref=planes.at[odd], dst_ref=gathered.at[me],
                    send_sem=plane_send.at[j], recv_sem=plane_recv.at[me],
                    device_id=(j, facing), device_id_type=MESH,
                )
                for j in partners
            ]
        return [
            pltpu.make_async_remote_copy(
                src_ref=src, dst_ref=dst, send_sem=plane_send.at[k], recv_sem=plane_recv.at[k],
                device_id=(partners[k], facing), device_id_type=MESH,
            )
            for k, (src, dst) in enumerate(
                ((planes.at[odd], gathered.at[0]), (edge_out, edge_in))
            )
        ]

    def side_copy(k, src, dst, device):
        return pltpu.make_async_remote_copy(
            src_ref=src, dst_ref=dst, send_sem=side_send.at[k], recv_sem=side_recv.at[k],
            device_id=device, device_id_type=MESH,
        )

    lane = lax.broadcasted_iota(jnp.int32, (axial, lanes), 1)
    row = lax.broadcasted_iota(jnp.int32, (axial, lanes), 0)

    def pack(r, held):
        place = jnp.logical_or(lane == 2 * r, lane == lax.rem(2 * r - 1 + lanes, lanes))
        return tuple(
            jnp.where(place, pltpu.roll(state[f, r], 2 * r, 1), held[f]) for f in range(5)
        )

    held = lax.fori_loop(
        0, radial, pack, tuple(jnp.ones((axial, lanes), jnp.float32) for _ in range(5)), unroll=8
    )
    even_lane = lax.rem(lane, 2) == 0
    low_lane = lane < lanes // 2

    place = [0, 1, lanes // 2, lanes // 2 + 1, 0]

    def dense(target, cols):
        rolled = [pltpu.roll(c, p, 1) if p else c for c, p in zip(cols, place)]
        target[0] = jnp.where(
            low_lane,
            jnp.where(even_lane, rolled[0], rolled[1]),
            jnp.where(even_lane, rolled[2], rolled[3]),
        )
        target[1] = rolled[4]

    dense(firsts, held)
    dense(lasts, [pltpu.roll(c, 1, 1) for c in held])

    if turn is not None:

        @pl.when(interface)
        def _():
            edge = jnp.zeros((radial, lanes), jnp.float32)
            for f in range(5):
                first = pltpu.roll(planes[0, f], f, 1)
                last = pltpu.roll(planes[1, f], f + 1, 1)
                edge = jnp.where(plane_lane == f, jnp.where(blk == 1, last, first), edge)
            edge_out[...] = edge

    not_last_row = row < axial - 1
    not_last_lane = lane < lanes - 1

    def cells(r):
        return tuple(state[f, r] for f in range(5))

    def step(r, carry):
        q, base, flux, reach, below = carry
        following = cells(jnp.minimum(r + 1, radial - 1))
        base_f = basics(following)
        flux_f, reach_f = flux_of(following, base_f, 2, RADIAL_COEF)
        above = between(q, flux, reach, following, flux_f, reach_f)
        total = [c - (a - b) for c, a, b in zip(q, above, below)]
        part = shifted_diff(q, base, 1, 0, not_last_row, AXIAL_COEF)
        total = [c - a for c, a in zip(total, part)]
        part = shifted_diff(q, base, 3, 1, not_last_lane, AROUND_COEF)
        for f in range(5):
            out[f, r] = total[f] - part[f]
        return following, base_f, tuple(flux_f), reach_f, tuple(above)

    q0 = cells(0)
    base0 = basics(q0)
    flux0, reach0 = flux_of(q0, base0, 2, RADIAL_COEF)
    first = between(q0, flux0, reach0, q0, flux0, reach0)
    carry = (q0, base0, tuple(flux0), reach0, tuple(first))
    carry = lax.fori_loop(0, radial // 8, step, carry, unroll=4)

    @pl.when(interface)
    def _():
        pl.semaphore_wait(barrier, 3 + len(partners))

    @pl.when(jnp.logical_not(interface))
    def _():
        pl.semaphore_wait(barrier, 3)

    to_mate = side_copy(0, planes.at[1 - odd], mate_in, (me, mate))
    to_ahead = side_copy(1, lasts, left_in, (ahead, blk))
    to_behind = side_copy(2, firsts, right_in, (behind, blk))
    to_ahead.start()
    to_behind.start()

    @pl.when(interface)
    def _():
        for copy in plane_copies():
            copy.start()

    to_mate.start()

    lax.fori_loop(radial // 8, radial, step, carry, unroll=4)

    def add_lower(beside):
        for start in range(0, radial, 8):
            rows = slice(start, start + 8)
            flux = face(
                [beside[f, rows] for f in range(5)], [planes[0, f, rows] for f in range(5)], 1, AXIAL_COEF
            )
            for f in range(5):
                out[f, rows, 0, :] = out[f, rows, 0, :] + flux[f]

    def add_upper(beside):
        for start in range(0, radial, 8):
            rows = slice(start, start + 8)
            flux = face(
                [planes[1, f, rows] for f in range(5)], [beside[f, rows] for f in range(5)], 1, AXIAL_COEF
            )
            for f in range(5):
                out[f, rows, axial - 1, :] = out[f, rows, axial - 1, :] - flux[f]

    to_mate.wait()

    @pl.when(odd == 0)
    def _():
        add_upper(mate_in)

    @pl.when(odd == 1)
    def _():
        add_lower(mate_in)

    to_ahead.wait()
    to_behind.wait()
    left = [
        jnp.where(even_lane, pltpu.roll(left_in[f // 4], (lanes - place[f]) % lanes, 1), held[f])
        for f in range(5)
    ]
    right = [
        jnp.where(even_lane, held[f], pltpu.roll(right_in[f // 4], lanes - 1 - place[f], 1))
        for f in range(5)
    ]
    sides = [jnp.where(even_lane, c, -c) for c in face(left, right, 3, AROUND_COEF)]
    ends = jnp.logical_or(lane == 0, lane == lanes - 1)

    def add_sides(r, _):
        for f in range(5):
            moved = pltpu.roll(sides[f], lax.rem(lanes - 2 * r, lanes), 1)
            out[f, r] = out[f, r] + jnp.where(ends, moved, 0.0)
        return 0

    lax.fori_loop(0, radial, add_sides, 0, unroll=8)

    for load in loads[5:]:
        load.wait()

    @pl.when(jnp.logical_not(interface))
    def _():
        outer[...] = planes[odd]

    @pl.when(interface)
    def _():
        if turn is None:
            for k in range(count):
                pltpu.make_async_remote_copy(
                    src_ref=planes.at[odd], dst_ref=gathered.at[k],
                    send_sem=plane_send.at[k], recv_sem=plane_recv.at[k],
                    device_id=(k, facing), device_id_type=MESH,
                ).wait()
        else:
            for copy in plane_copies():
                copy.wait()
        weights = jnp.zeros((1, lanes), jnp.float32)
        for k in range(table.shape[0]):
            weights = jnp.where(stencil[...] == k, table[k], weights)
        offset = 0 if turn is not None else lax.rem(partner[me] - me + count, count)

        def ghost(main_at, edge_at, shift, edge_lane):
            for f in range(5):
                main = gathered[0, f] if turn is not None else gathered[main_at, f]
                if turn is not None:
                    edge = pltpu.roll(edge_in[...], (edge_lane - f) % lanes, 1)
                else:
                    edge = pltpu.roll(gathered[edge_at, f], shift, 1)
                beside = jnp.where(plane_lane == edge_lane, edge, pltpu.roll(main, shift, 1))
                outer[f] = weights * main + (1.0 - weights) * beside

        @pl.when(blk == 1)
        def _():
            at = lax.rem(me + offset, count)
            ghost(at, lax.rem(at + 1, count), lanes - 1, lanes - 1)

        @pl.when(blk == 2)
        def _():
            at = lax.rem(me - offset + count, count)
            ghost(at, lax.rem(at + count - 1, count), 1, 0)

    @pl.when(odd == 0)
    def _():
        add_lower(outer)

    @pl.when(odd == 1)
    def _():
        add_upper(outer)


def section(turn, state, partner, stencil, weight_table):
    count = lax.axis_size("pass")
    _, radial, axial, lanes = state.shape
    hbm = pl.BlockSpec(memory_space=pltpu.HBM)
    f32 = jnp.float32
    held = count if turn is None else 1
    copies = count if turn is None else 2
    return pl.pallas_call(
        functools.partial(kernel, count, turn),
        out_shape=jax.ShapeDtypeStruct(state.shape, f32),
        in_specs=[hbm] * 4,
        out_specs=pl.BlockSpec(memory_space=pltpu.VMEM),
        scratch_shapes=[
            pltpu.VMEM(state.shape, f32),
            pltpu.SMEM(partner.shape, jnp.int32),
            pltpu.VMEM(stencil.shape, jnp.int32),
            pltpu.SMEM(weight_table.shape, f32),
            pltpu.VMEM((2, 5, radial, lanes), f32),
            pltpu.VMEM((5, radial, lanes), f32),
            pltpu.VMEM((held, 5, radial, lanes), f32),
            pltpu.VMEM((radial, lanes), f32),
            pltpu.VMEM((radial, lanes), f32),
            pltpu.VMEM((5, radial, lanes), f32),
            pltpu.VMEM((2, axial, lanes), f32),
            pltpu.VMEM((2, axial, lanes), f32),
            pltpu.VMEM((2, axial, lanes), f32),
            pltpu.VMEM((2, axial, lanes), f32),
            pltpu.SemaphoreType.DMA((copies,)),
            pltpu.SemaphoreType.DMA((copies,)),
            pltpu.SemaphoreType.DMA((3,)),
            pltpu.SemaphoreType.DMA((3,)),
            pltpu.SemaphoreType.DMA((8,)),
        ],
        compiler_params=pltpu.CompilerParams(
            collective_id=turn or 0, has_side_effects=True, vmem_limit_bytes=24 * 1024 * 1024
        ),
        cost_estimate=pl.CostEstimate(
            flops=200 * radial * axial * lanes, bytes_accessed=8 * state.size, transcendentals=0
        ),
    )(state, partner, stencil, weight_table)


def store_kernel(value, out, sem):
    half = value.shape[1] // 2
    copies = [
        pltpu.make_async_copy(
            value.at[f, pl.ds(h * half, half)], out.at[f, pl.ds(h * half, half)], sem.at[f, h]
        )
        for f in range(5)
        for h in range(2)
    ]
    for copy in copies:
        copy.start()
    for copy in copies:
        copy.wait()


def store(value):
    return pl.pallas_call(
        store_kernel,
        out_shape=jax.ShapeDtypeStruct(value.shape, value.dtype),
        in_specs=[pl.BlockSpec(memory_space=pltpu.VMEM)],
        out_specs=pl.BlockSpec(memory_space=pltpu.HBM),
        scratch_shapes=[pltpu.SemaphoreType.DMA((5, 2))],
        compiler_params=pltpu.CompilerParams(vmem_limit_bytes=24 * 1024 * 1024),
    )(value)


def shards(state, partner, stencil, weight_table):
    count = lax.axis_size("pass")
    operands = (state, partner, stencil.reshape(1, -1), weight_table)
    if count > 8:
        return store(section(None, *operands))
    value = lax.switch(
        partner[0] - 1, [functools.partial(section, k) for k in range(1, count)], *operands
    )
    return store(value)


def solution(mesh):
    placed = (P(None, None, "blk", "pass"), P(), P("pass"), P())
    return jax.shard_map(
        shards, mesh=mesh, in_specs=placed, out_specs=P(None, None, "blk", "pass"), check_vma=False
    )
```

```python
import functools

import jax
import jax.numpy as jnp
from jax import lax
from jax.experimental import pallas as pl
from jax.experimental.pallas import tpu as pltpu
from jax.sharding import PartitionSpec as P

AXIAL_COEF = 0.4
RADIAL_COEF = 0.3
AROUND_COEF = 0.3
MESH = pl.DeviceIdType.MESH


def basics(q):
    inv = 1.0 / q[0]
    pressure = 0.4 * (q[4] - 0.5 * (q[1] * q[1] + q[2] * q[2] + q[3] * q[3]) * inv)
    square = 1.4 * pressure * inv
    return inv, pressure, square * lax.rsqrt(square)


def flux_of(q, base, d, scale):
    inv, pressure, sound = base
    u = q[d] * (inv * (0.5 * scale))
    part = pressure * (0.5 * scale)
    flux = [c * u for c in q]
    flux[d] = flux[d] + part
    flux[4] = flux[4] + pressure * u
    return flux, jnp.abs(u) + sound * (0.5 * scale)


def between(left, flux_left, reach_left, right, flux_right, reach_right):
    reach = jnp.maximum(reach_left, reach_right)
    return [
        (fl + fr) - reach * (b - a)
        for a, fl, b, fr in zip(left, flux_left, right, flux_right)
    ]


def face(left, right, d, scale):
    fl, rl = flux_of(left, basics(left), d, scale)
    fr, rr = flux_of(right, basics(right), d, scale)
    return between(left, fl, rl, right, fr, rr)


def shifted_diff(q, base, d, axis, keep, scale):
    length = q[0].shape[axis]
    up = lambda x: pltpu.roll(x, length - 1, axis)
    flux, reach = flux_of(q, base, d, scale)
    above = between(q, flux, reach, [up(c) for c in q], [up(c) for c in flux], up(reach))
    above = [jnp.where(keep, c, 0.0) for c in above]
    return [c - pltpu.roll(c, 1, axis) for c in above]


def kernel(
    count, turn, state_in, partner_in, stencil_in, table_in, out, sides_out, lower_out, upper_out,
    state, partner, stencil, table,
    planes, mate_in, gathered, edge_out, edge_in, outer, firsts, lasts, left_in, right_in,
    plane_send, plane_recv, side_send, side_recv, load_sem,
):
    me = lax.axis_index("pass")
    blk = lax.axis_index("blk")
    odd = lax.rem(blk, 2)
    mate = blk + 1 - 2 * odd
    facing = 3 - blk
    ahead, behind = lax.rem(me + 1, count), lax.rem(me + count - 1, count)
    radial, axial, lanes = state.shape[1:]
    interface = jnp.logical_or(blk == 1, blk == 2)
    if turn is None:
        partners = list(range(count))
    else:
        sign = jnp.where(blk == 1, 1, -1)
        partners = [lax.rem(me + sign * (turn + k) + 2 * count, count) for k in range(2)]

    loads = [pltpu.make_async_copy(state_in.at[f], state.at[f], load_sem.at[f]) for f in range(5)]
    loads.append(pltpu.make_async_copy(stencil_in, stencil, load_sem.at[5]))
    loads.append(pltpu.make_async_copy(table_in, table, load_sem.at[6]))
    if turn is None:
        loads.append(pltpu.make_async_copy(partner_in, partner, load_sem.at[7]))
    for load in loads:
        load.start()

    barrier = pltpu.get_barrier_semaphore()
    for device in ((ahead, blk), (behind, blk), (me, mate)):
        pl.semaphore_signal(barrier, inc=1, device_id=device, device_id_type=MESH)

    @pl.when(interface)
    def _():
        for j in partners:
            pl.semaphore_signal(barrier, inc=1, device_id=(j, facing), device_id_type=MESH)

    for f in range(5):
        loads[f].wait()
        planes[0, f] = state[f, :, 0, :]
        planes[1, f] = state[f, :, axial - 1, :]
    plane_lane = lax.broadcasted_iota(jnp.int32, (radial, lanes), 1)

    def plane_copies():
        if turn is None:
            return [
                pltpu.make_async_remote_copy(
                    src_ref=planes.at[odd], dst_ref=gathered.at[me],
                    send_sem=plane_send.at[j], recv_sem=plane_recv.at[me],
                    device_id=(j, facing), device_id_type=MESH,
                )
                for j in partners
            ]
        return [
            pltpu.make_async_remote_copy(
                src_ref=src, dst_ref=dst, send_sem=plane_send.at[k], recv_sem=plane_recv.at[k],
                device_id=(partners[k], facing), device_id_type=MESH,
            )
            for k, (src, dst) in enumerate(
                ((planes.at[odd], gathered.at[0]), (edge_out, edge_in))
            )
        ]

    def side_copy(k, src, dst, device):
        return pltpu.make_async_remote_copy(
            src_ref=src, dst_ref=dst, send_sem=side_send.at[k], recv_sem=side_recv.at[k],
            device_id=device, device_id_type=MESH,
        )

    lane = lax.broadcasted_iota(jnp.int32, (axial, lanes), 1)
    row = lax.broadcasted_iota(jnp.int32, (axial, lanes), 0)

    def pack(r, held):
        place = jnp.logical_or(lane == 2 * r, lane == lax.rem(2 * r - 1 + lanes, lanes))
        return tuple(
            jnp.where(place, pltpu.roll(state[f, r], 2 * r, 1), held[f]) for f in range(5)
        )

    held = lax.fori_loop(
        0, radial, pack, tuple(jnp.ones((axial, lanes), jnp.float32) for _ in range(5)), unroll=8
    )
    even_lane = lax.rem(lane, 2) == 0
    low_lane = lane < lanes // 2

    place = [0, 1, lanes // 2, lanes // 2 + 1, 0]

    def dense(target, cols):
        rolled = [pltpu.roll(c, p, 1) if p else c for c, p in zip(cols, place)]
        target[0] = jnp.where(
            low_lane,
            jnp.where(even_lane, rolled[0], rolled[1]),
            jnp.where(even_lane, rolled[2], rolled[3]),
        )
        target[1] = rolled[4]

    dense(firsts, held)
    dense(lasts, [pltpu.roll(c, 1, 1) for c in held])

    if turn is not None:

        @pl.when(interface)
        def _():
            edge = jnp.zeros((radial, lanes), jnp.float32)
            for f in range(5):
                first = pltpu.roll(planes[0, f], f, 1)
                last = pltpu.roll(planes[1, f], f + 1, 1)
                edge = jnp.where(plane_lane == f, jnp.where(blk == 1, last, first), edge)
            edge_out[...] = edge

    not_last_row = row < axial - 1
    not_last_lane = lane < lanes - 1

    def cells(r):
        return tuple(state[f, r] for f in range(5))

    def step(r, carry):
        q, base, flux, reach, below = carry
        following = cells(jnp.minimum(r + 1, radial - 1))
        base_f = basics(following)
        flux_f, reach_f = flux_of(following, base_f, 2, RADIAL_COEF)
        above = between(q, flux, reach, following, flux_f, reach_f)
        total = [c - (a - b) for c, a, b in zip(q, above, below)]
        part = shifted_diff(q, base, 1, 0, not_last_row, AXIAL_COEF)
        total = [c - a for c, a in zip(total, part)]
        part = shifted_diff(q, base, 3, 1, not_last_lane, AROUND_COEF)
        for f in range(5):
            out[f, r] = total[f] - part[f]
        return following, base_f, tuple(flux_f), reach_f, tuple(above)

    q0 = cells(0)
    base0 = basics(q0)
    flux0, reach0 = flux_of(q0, base0, 2, RADIAL_COEF)
    first = between(q0, flux0, reach0, q0, flux0, reach0)
    carry = (q0, base0, tuple(flux0), reach0, tuple(first))
    carry = lax.fori_loop(0, radial // 8, step, carry, unroll=4)

    @pl.when(interface)
    def _():
        pl.semaphore_wait(barrier, 3 + len(partners))

    @pl.when(jnp.logical_not(interface))
    def _():
        pl.semaphore_wait(barrier, 3)

    to_mate = side_copy(0, planes.at[1 - odd], mate_in, (me, mate))
    to_ahead = side_copy(1, lasts, left_in, (ahead, blk))
    to_behind = side_copy(2, firsts, right_in, (behind, blk))
    to_ahead.start()
    to_behind.start()

    @pl.when(interface)
    def _():
        for copy in plane_copies():
            copy.start()

    to_mate.start()

    lax.fori_loop(radial // 8, radial, step, carry, unroll=4)

    def lower_faces(beside):
        for start in range(0, radial, 8):
            rows = slice(start, start + 8)
            flux = face(
                [beside[f, rows] for f in range(5)], [planes[0, f, rows] for f in range(5)], 1, AXIAL_COEF
            )
            for f in range(5):
                lower_out[f, rows] = flux[f]

    def upper_faces(beside):
        for start in range(0, radial, 8):
            rows = slice(start, start + 8)
            flux = face(
                [planes[1, f, rows] for f in range(5)], [beside[f, rows] for f in range(5)], 1, AXIAL_COEF
            )
            for f in range(5):
                upper_out[f, rows] = flux[f]

    to_mate.wait()

    @pl.when(odd == 0)
    def _():
        upper_faces(mate_in)

    @pl.when(odd == 1)
    def _():
        lower_faces(mate_in)

    to_ahead.wait()
    to_behind.wait()
    left = [
        jnp.where(even_lane, pltpu.roll(left_in[f // 4], (lanes - place[f]) % lanes, 1), held[f])
        for f in range(5)
    ]
    right = [
        jnp.where(even_lane, held[f], pltpu.roll(right_in[f // 4], lanes - 1 - place[f], 1))
        for f in range(5)
    ]
    sides = face(left, right, 3, AROUND_COEF)
    for f in range(5):
        sides_out[f] = jnp.where(even_lane, sides[f], -sides[f])

    for load in loads[5:]:
        load.wait()

    @pl.when(jnp.logical_not(interface))
    def _():
        outer[...] = planes[odd]

    @pl.when(interface)
    def _():
        if turn is None:
            for k in range(count):
                pltpu.make_async_remote_copy(
                    src_ref=planes.at[odd], dst_ref=gathered.at[k],
                    send_sem=plane_send.at[k], recv_sem=plane_recv.at[k],
                    device_id=(k, facing), device_id_type=MESH,
                ).wait()
        else:
            for copy in plane_copies():
                copy.wait()
        weights = jnp.zeros((1, lanes), jnp.float32)
        for k in range(table.shape[0]):
            weights = jnp.where(stencil[...] == k, table[k], weights)
        offset = 0 if turn is not None else lax.rem(partner[me] - me + count, count)

        def ghost(main_at, edge_at, shift, edge_lane):
            for f in range(5):
                main = gathered[0, f] if turn is not None else gathered[main_at, f]
                if turn is not None:
                    edge = pltpu.roll(edge_in[...], (edge_lane - f) % lanes, 1)
                else:
                    edge = pltpu.roll(gathered[edge_at, f], shift, 1)
                beside = jnp.where(plane_lane == edge_lane, edge, pltpu.roll(main, shift, 1))
                outer[f] = weights * main + (1.0 - weights) * beside

        @pl.when(blk == 1)
        def _():
            at = lax.rem(me + offset, count)
            ghost(at, lax.rem(at + 1, count), lanes - 1, lanes - 1)

        @pl.when(blk == 2)
        def _():
            at = lax.rem(me - offset + count, count)
            ghost(at, lax.rem(at + count - 1, count), 1, 0)

    @pl.when(odd == 0)
    def _():
        lower_faces(outer)

    @pl.when(odd == 1)
    def _():
        upper_faces(outer)


def section(turn, state, partner, stencil, weight_table):
    count = lax.axis_size("pass")
    _, radial, axial, lanes = state.shape
    hbm = pl.BlockSpec(memory_space=pltpu.HBM)
    f32 = jnp.float32
    held = count if turn is None else 1
    copies = count if turn is None else 2
    return pl.pallas_call(
        functools.partial(kernel, count, turn),
        out_shape=[
            jax.ShapeDtypeStruct(shape, f32)
            for shape in (state.shape, (5, axial, lanes), (5, radial, lanes), (5, radial, lanes))
        ],
        in_specs=[hbm] * 4,
        out_specs=[pl.BlockSpec(memory_space=pltpu.VMEM)] * 4,
        scratch_shapes=[
            pltpu.VMEM(state.shape, f32),
            pltpu.SMEM(partner.shape, jnp.int32),
            pltpu.VMEM(stencil.shape, jnp.int32),
            pltpu.SMEM(weight_table.shape, f32),
            pltpu.VMEM((2, 5, radial, lanes), f32),
            pltpu.VMEM((5, radial, lanes), f32),
            pltpu.VMEM((held, 5, radial, lanes), f32),
            pltpu.VMEM((radial, lanes), f32),
            pltpu.VMEM((radial, lanes), f32),
            pltpu.VMEM((5, radial, lanes), f32),
            pltpu.VMEM((2, axial, lanes), f32),
            pltpu.VMEM((2, axial, lanes), f32),
            pltpu.VMEM((2, axial, lanes), f32),
            pltpu.VMEM((2, axial, lanes), f32),
            pltpu.SemaphoreType.DMA((copies,)),
            pltpu.SemaphoreType.DMA((copies,)),
            pltpu.SemaphoreType.DMA((3,)),
            pltpu.SemaphoreType.DMA((3,)),
            pltpu.SemaphoreType.DMA((8,)),
        ],
        compiler_params=pltpu.CompilerParams(
            collective_id=turn or 0, has_side_effects=True, vmem_limit_bytes=24 * 1024 * 1024
        ),
        cost_estimate=pl.CostEstimate(
            flops=200 * radial * axial * lanes, bytes_accessed=8 * state.size, transcendentals=0
        ),
    )(state, partner, stencil, weight_table)


def store_kernel(value, sides, lower, upper, out, held, sem):
    _, radial, axial, lanes = value.shape
    lane = lax.broadcasted_iota(jnp.int32, (axial, lanes), 1)
    ends = jnp.logical_or(lane == 0, lane == lanes - 1)
    copies = []
    for start in range(0, radial, 8):
        rows = slice(start, start + 8)
        for f in range(5):
            for r in range(start, start + 8):
                moved = pltpu.roll(sides[f], (lanes - 2 * r) % lanes, 1) if r else sides[f]
                held[f, r] = value[f, r] + jnp.where(ends, moved, 0.0)
            held[f, rows, 0, :] = held[f, rows, 0, :] + lower[f, rows]
            held[f, rows, axial - 1, :] = held[f, rows, axial - 1, :] - upper[f, rows]
            copy = pltpu.make_async_copy(
                held.at[f, pl.ds(start, 8)], out.at[f, pl.ds(start, 8)], sem.at[start // 8, f]
            )
            copy.start()
            copies.append(copy)
    for copy in copies:
        copy.wait()


def store(value, sides, lower, upper):
    return pl.pallas_call(
        store_kernel,
        out_shape=jax.ShapeDtypeStruct(value.shape, value.dtype),
        in_specs=[pl.BlockSpec(memory_space=pltpu.VMEM)] * 4,
        out_specs=pl.BlockSpec(memory_space=pltpu.HBM),
        scratch_shapes=[
            pltpu.VMEM(value.shape, value.dtype),
            pltpu.SemaphoreType.DMA((value.shape[1] // 8, 5)),
        ],
        compiler_params=pltpu.CompilerParams(vmem_limit_bytes=24 * 1024 * 1024),
    )(value, sides, lower, upper)


def shards(state, partner, stencil, weight_table):
    count = lax.axis_size("pass")
    operands = (state, partner, stencil.reshape(1, -1), weight_table)
    if count > 8:
        return store(*section(None, *operands))
    parts = lax.switch(
        partner[0] - 1, [functools.partial(section, k) for k in range(1, count)], *operands
    )
    return store(*parts)


def solution(mesh):
    placed = (P(None, None, "blk", "pass"), P(), P("pass"), P())
    return jax.shard_map(
        shards, mesh=mesh, in_specs=placed, out_specs=P(None, None, "blk", "pass"), check_vma=False
    )
```

```python
import functools

import jax
import jax.numpy as jnp
from jax import lax
from jax.experimental import pallas as pl
from jax.experimental.pallas import tpu as pltpu
from jax.sharding import PartitionSpec as P

AXIAL_COEF = 0.4
RADIAL_COEF = 0.3
AROUND_COEF = 0.3
MESH = pl.DeviceIdType.MESH


def basics(q):
    inv = 1.0 / q[0]
    pressure = 0.4 * (q[4] - 0.5 * (q[1] * q[1] + q[2] * q[2] + q[3] * q[3]) * inv)
    square = 1.4 * pressure * inv
    return inv, pressure, square * lax.rsqrt(square)


def flux_of(q, base, d, scale):
    inv, pressure, sound = base
    u = q[d] * (inv * (0.5 * scale))
    part = pressure * (0.5 * scale)
    flux = [c * u for c in q]
    flux[d] = flux[d] + part
    flux[4] = flux[4] + pressure * u
    return flux, jnp.abs(u) + sound * (0.5 * scale)


def between(left, flux_left, reach_left, right, flux_right, reach_right):
    reach = jnp.maximum(reach_left, reach_right)
    return [
        (fl + fr) - reach * (b - a)
        for a, fl, b, fr in zip(left, flux_left, right, flux_right)
    ]


def face(left, right, d, scale):
    fl, rl = flux_of(left, basics(left), d, scale)
    fr, rr = flux_of(right, basics(right), d, scale)
    return between(left, fl, rl, right, fr, rr)


def shifted_diff(q, base, d, axis, keep, scale):
    length = q[0].shape[axis]
    up = lambda x: pltpu.roll(x, length - 1, axis)
    flux, reach = flux_of(q, base, d, scale)
    above = between(q, flux, reach, [up(c) for c in q], [up(c) for c in flux], up(reach))
    above = [jnp.where(keep, c, 0.0) for c in above]
    return [c - pltpu.roll(c, 1, axis) for c in above]


def kernel(
    count, turn, state_in, partner_in, stencil_in, table_in, out, sides_out, lower_out, upper_out,
    state, partner, stencil, table,
    planes, mate_in, gathered, edge_out, edge_in, outer, firsts, lasts, left_in, right_in,
    plane_send, plane_recv, side_send, side_recv, load_sem,
):
    me = lax.axis_index("pass")
    blk = lax.axis_index("blk")
    odd = lax.rem(blk, 2)
    mate = blk + 1 - 2 * odd
    facing = 3 - blk
    ahead, behind = lax.rem(me + 1, count), lax.rem(me + count - 1, count)
    radial, axial, lanes = state.shape[1:]
    interface = jnp.logical_or(blk == 1, blk == 2)
    if turn is None:
        partners = list(range(count))
    else:
        sign = jnp.where(blk == 1, 1, -1)
        partners = [lax.rem(me + sign * (turn + k) + 2 * count, count) for k in range(2)]

    loads = [pltpu.make_async_copy(state_in.at[f], state.at[f], load_sem.at[f]) for f in range(5)]
    loads.append(pltpu.make_async_copy(stencil_in, stencil, load_sem.at[5]))
    loads.append(pltpu.make_async_copy(table_in, table, load_sem.at[6]))
    if turn is None:
        loads.append(pltpu.make_async_copy(partner_in, partner, load_sem.at[7]))
    for load in loads:
        load.start()

    barrier = pltpu.get_barrier_semaphore()
    for device in ((ahead, blk), (behind, blk), (me, mate)):
        pl.semaphore_signal(barrier, inc=1, device_id=device, device_id_type=MESH)

    @pl.when(interface)
    def _():
        for j in partners:
            pl.semaphore_signal(barrier, inc=1, device_id=(j, facing), device_id_type=MESH)

    for f in range(5):
        loads[f].wait()
        planes[0, f] = state[f, :, 0, :]
        planes[1, f] = state[f, :, axial - 1, :]
    plane_lane = lax.broadcasted_iota(jnp.int32, (radial, lanes), 1)

    def plane_copies():
        if turn is None:
            return [
                pltpu.make_async_remote_copy(
                    src_ref=planes.at[odd], dst_ref=gathered.at[me],
                    send_sem=plane_send.at[j], recv_sem=plane_recv.at[me],
                    device_id=(j, facing), device_id_type=MESH,
                )
                for j in partners
            ]
        pairs = [(planes.at[odd, f], gathered.at[0, f]) for f in range(5)] + [(edge_out, edge_in)]
        return [
            pltpu.make_async_remote_copy(
                src_ref=src, dst_ref=dst, send_sem=plane_send.at[k], recv_sem=plane_recv.at[k],
                device_id=(partners[k // 5], facing), device_id_type=MESH,
            )
            for k, (src, dst) in enumerate(pairs)
        ]

    def side_copy(k, src, dst, device):
        return pltpu.make_async_remote_copy(
            src_ref=src, dst_ref=dst, send_sem=side_send.at[k], recv_sem=side_recv.at[k],
            device_id=device, device_id_type=MESH,
        )

    @pl.when(interface)
    def _():
        pl.semaphore_wait(barrier, 3 + len(partners))
        copies = plane_copies()
        for copy in copies if turn is None else copies[:5]:
            copy.start()
        if turn is not None:
            edge = jnp.zeros((radial, lanes), jnp.float32)
            for f in range(5):
                first = pltpu.roll(planes[0, f], f, 1)
                last = pltpu.roll(planes[1, f], f + 1, 1)
                edge = jnp.where(plane_lane == f, jnp.where(blk == 1, last, first), edge)
            edge_out[...] = edge
            copies[5].start()

    @pl.when(jnp.logical_not(interface))
    def _():
        pl.semaphore_wait(barrier, 3)

    to_mate = side_copy(0, planes.at[1 - odd], mate_in, (me, mate))
    to_ahead = side_copy(1, lasts, left_in, (ahead, blk))
    to_behind = side_copy(2, firsts, right_in, (behind, blk))
    to_mate.start()

    lane = lax.broadcasted_iota(jnp.int32, (axial, lanes), 1)
    row = lax.broadcasted_iota(jnp.int32, (axial, lanes), 0)

    def pack(r, held):
        place = jnp.logical_or(lane == 2 * r, lane == lax.rem(2 * r - 1 + lanes, lanes))
        return tuple(
            jnp.where(place, pltpu.roll(state[f, r], 2 * r, 1), held[f]) for f in range(5)
        )

    held = lax.fori_loop(
        0, radial, pack, tuple(jnp.ones((axial, lanes), jnp.float32) for _ in range(5)), unroll=8
    )
    even_lane = lax.rem(lane, 2) == 0
    low_lane = lane < lanes // 2

    place = [0, 1, lanes // 2, lanes // 2 + 1, 0]

    def dense(target, cols):
        rolled = [pltpu.roll(c, p, 1) if p else c for c, p in zip(cols, place)]
        target[0] = jnp.where(
            low_lane,
            jnp.where(even_lane, rolled[0], rolled[1]),
            jnp.where(even_lane, rolled[2], rolled[3]),
        )
        target[1] = rolled[4]

    dense(firsts, held)
    dense(lasts, [pltpu.roll(c, 1, 1) for c in held])
    to_ahead.start()
    to_behind.start()

    not_last_row = row < axial - 1
    not_last_lane = lane < lanes - 1

    def cells(r):
        return tuple(state[f, r] for f in range(5))

    def step(r, carry):
        q, base, flux, reach, below = carry
        following = cells(jnp.minimum(r + 1, radial - 1))
        base_f = basics(following)
        flux_f, reach_f = flux_of(following, base_f, 2, RADIAL_COEF)
        above = between(q, flux, reach, following, flux_f, reach_f)
        total = [c - (a - b) for c, a, b in zip(q, above, below)]
        part = shifted_diff(q, base, 1, 0, not_last_row, AXIAL_COEF)
        total = [c - a for c, a in zip(total, part)]
        part = shifted_diff(q, base, 3, 1, not_last_lane, AROUND_COEF)
        for f in range(5):
            out[f, r] = total[f] - part[f]
        return following, base_f, tuple(flux_f), reach_f, tuple(above)

    q0 = cells(0)
    base0 = basics(q0)
    flux0, reach0 = flux_of(q0, base0, 2, RADIAL_COEF)
    first = between(q0, flux0, reach0, q0, flux0, reach0)
    carry = (q0, base0, tuple(flux0), reach0, tuple(first))
    lax.fori_loop(0, radial, step, carry, unroll=4)

    def lower_faces(beside):
        for start in range(0, radial, 8):
            rows = slice(start, start + 8)
            flux = face(
                [beside[f, rows] for f in range(5)], [planes[0, f, rows] for f in range(5)], 1, AXIAL_COEF
            )
            for f in range(5):
                lower_out[f, rows] = flux[f]

    def upper_faces(beside):
        for start in range(0, radial, 8):
            rows = slice(start, start + 8)
            flux = face(
                [planes[1, f, rows] for f in range(5)], [beside[f, rows] for f in range(5)], 1, AXIAL_COEF
            )
            for f in range(5):
                upper_out[f, rows] = flux[f]

    to_mate.wait()

    @pl.when(odd == 0)
    def _():
        upper_faces(mate_in)

    @pl.when(odd == 1)
    def _():
        lower_faces(mate_in)

    to_ahead.wait()
    to_behind.wait()
    left = [
        jnp.where(even_lane, pltpu.roll(left_in[f // 4], (lanes - place[f]) % lanes, 1), held[f])
        for f in range(5)
    ]
    right = [
        jnp.where(even_lane, held[f], pltpu.roll(right_in[f // 4], lanes - 1 - place[f], 1))
        for f in range(5)
    ]
    sides = face(left, right, 3, AROUND_COEF)
    for f in range(5):
        sides_out[f] = jnp.where(even_lane, sides[f], -sides[f])

    for load in loads[5:]:
        load.wait()

    @pl.when(jnp.logical_not(interface))
    def _():
        outer[...] = planes[odd]

    @pl.when(interface)
    def _():
        if turn is None:
            for k in range(count):
                pltpu.make_async_remote_copy(
                    src_ref=planes.at[odd], dst_ref=gathered.at[k],
                    send_sem=plane_send.at[k], recv_sem=plane_recv.at[k],
                    device_id=(k, facing), device_id_type=MESH,
                ).wait()
        else:
            for copy in plane_copies():
                copy.wait()
        weights = jnp.zeros((1, lanes), jnp.float32)
        for k in range(table.shape[0]):
            weights = jnp.where(stencil[...] == k, table[k], weights)
        offset = 0 if turn is not None else lax.rem(partner[me] - me + count, count)

        def ghost(main_at, edge_at, shift, edge_lane):
            for f in range(5):
                main = gathered[0, f] if turn is not None else gathered[main_at, f]
                if turn is not None:
                    edge = pltpu.roll(edge_in[...], (edge_lane - f) % lanes, 1)
                else:
                    edge = pltpu.roll(gathered[edge_at, f], shift, 1)
                beside = jnp.where(plane_lane == edge_lane, edge, pltpu.roll(main, shift, 1))
                outer[f] = weights * main + (1.0 - weights) * beside

        @pl.when(blk == 1)
        def _():
            at = lax.rem(me + offset, count)
            ghost(at, lax.rem(at + 1, count), lanes - 1, lanes - 1)

        @pl.when(blk == 2)
        def _():
            at = lax.rem(me - offset + count, count)
            ghost(at, lax.rem(at + count - 1, count), 1, 0)

    @pl.when(odd == 0)
    def _():
        lower_faces(outer)

    @pl.when(odd == 1)
    def _():
        upper_faces(outer)


def section(turn, state, partner, stencil, weight_table):
    count = lax.axis_size("pass")
    _, radial, axial, lanes = state.shape
    hbm = pl.BlockSpec(memory_space=pltpu.HBM)
    f32 = jnp.float32
    held = count if turn is None else 1
    copies = count if turn is None else 6
    return pl.pallas_call(
        functools.partial(kernel, count, turn),
        out_shape=[
            jax.ShapeDtypeStruct(shape, f32)
            for shape in (state.shape, (5, axial, lanes), (5, radial, lanes), (5, radial, lanes))
        ],
        in_specs=[hbm] * 4,
        out_specs=[pl.BlockSpec(memory_space=pltpu.VMEM)] * 4,
        scratch_shapes=[
            pltpu.VMEM(state.shape, f32),
            pltpu.SMEM(partner.shape, jnp.int32),
            pltpu.VMEM(stencil.shape, jnp.int32),
            pltpu.SMEM(weight_table.shape, f32),
            pltpu.VMEM((2, 5, radial, lanes), f32),
            pltpu.VMEM((5, radial, lanes), f32),
            pltpu.VMEM((held, 5, radial, lanes), f32),
            pltpu.VMEM((radial, lanes), f32),
            pltpu.VMEM((radial, lanes), f32),
            pltpu.VMEM((5, radial, lanes), f32),
            pltpu.VMEM((2, axial, lanes), f32),
            pltpu.VMEM((2, axial, lanes), f32),
            pltpu.VMEM((2, axial, lanes), f32),
            pltpu.VMEM((2, axial, lanes), f32),
            pltpu.SemaphoreType.DMA((copies,)),
            pltpu.SemaphoreType.DMA((copies,)),
            pltpu.SemaphoreType.DMA((3,)),
            pltpu.SemaphoreType.DMA((3,)),
            pltpu.SemaphoreType.DMA((8,)),
        ],
        compiler_params=pltpu.CompilerParams(
            collective_id=turn or 0, has_side_effects=True, vmem_limit_bytes=24 * 1024 * 1024
        ),
        cost_estimate=pl.CostEstimate(
            flops=200 * radial * axial * lanes, bytes_accessed=8 * state.size, transcendentals=0
        ),
    )(state, partner, stencil, weight_table)


def store_kernel(value, sides, lower, upper, out, held, sem):
    _, radial, axial, lanes = value.shape
    lane = lax.broadcasted_iota(jnp.int32, (axial, lanes), 1)
    ends = jnp.logical_or(lane == 0, lane == lanes - 1)
    copies = []
    for start in range(0, radial, 8):
        rows = slice(start, start + 8)
        for f in range(5):
            for r in range(start, start + 8):
                moved = pltpu.roll(sides[f], (lanes - 2 * r) % lanes, 1) if r else sides[f]
                held[f, r] = value[f, r] + jnp.where(ends, moved, 0.0)
            held[f, rows, 0, :] = held[f, rows, 0, :] + lower[f, rows]
            held[f, rows, axial - 1, :] = held[f, rows, axial - 1, :] - upper[f, rows]
            copy = pltpu.make_async_copy(
                held.at[f, pl.ds(start, 8)], out.at[f, pl.ds(start, 8)], sem.at[start // 8, f]
            )
            copy.start()
            copies.append(copy)
    for copy in copies:
        copy.wait()


def store(value, sides, lower, upper):
    return pl.pallas_call(
        store_kernel,
        out_shape=jax.ShapeDtypeStruct(value.shape, value.dtype),
        in_specs=[pl.BlockSpec(memory_space=pltpu.VMEM)] * 4,
        out_specs=pl.BlockSpec(memory_space=pltpu.HBM),
        scratch_shapes=[
            pltpu.VMEM(value.shape, value.dtype),
            pltpu.SemaphoreType.DMA((value.shape[1] // 8, 5)),
        ],
        compiler_params=pltpu.CompilerParams(vmem_limit_bytes=24 * 1024 * 1024),
    )(value, sides, lower, upper)


def shards(state, partner, stencil, weight_table):
    count = lax.axis_size("pass")
    operands = (state, partner, stencil.reshape(1, -1), weight_table)
    if count > 8:
        return store(*section(None, *operands))
    parts = lax.switch(
        partner[0] - 1, [functools.partial(section, k) for k in range(1, count)], *operands
    )
    return store(*parts)


def solution(mesh):
    placed = (P(None, None, "blk", "pass"), P(), P("pass"), P())
    return jax.shard_map(
        shards, mesh=mesh, in_specs=placed, out_specs=P(None, None, "blk", "pass"), check_vma=False
    )
```

```python
import functools

import jax
import jax.numpy as jnp
from jax import lax
from jax.experimental import pallas as pl
from jax.experimental.pallas import tpu as pltpu
from jax.sharding import PartitionSpec as P

AXIAL_COEF = 0.4
RADIAL_COEF = 0.3
AROUND_COEF = 0.3
MESH = pl.DeviceIdType.MESH


def basics(q):
    inv = 1.0 / q[0]
    pressure = 0.4 * (q[4] - 0.5 * (q[1] * q[1] + q[2] * q[2] + q[3] * q[3]) * inv)
    square = 1.4 * pressure * inv
    return inv, pressure, square * lax.rsqrt(square)


def flux_of(q, base, d, scale):
    inv, pressure, sound = base
    u = q[d] * (inv * (0.5 * scale))
    part = pressure * (0.5 * scale)
    flux = [c * u for c in q]
    flux[d] = flux[d] + part
    flux[4] = flux[4] + pressure * u
    return flux, jnp.abs(u) + sound * (0.5 * scale)


def between(left, flux_left, reach_left, right, flux_right, reach_right):
    reach = jnp.maximum(reach_left, reach_right)
    return [
        (fl + fr) - reach * (b - a)
        for a, fl, b, fr in zip(left, flux_left, right, flux_right)
    ]


def face(left, right, d, scale):
    fl, rl = flux_of(left, basics(left), d, scale)
    fr, rr = flux_of(right, basics(right), d, scale)
    return between(left, fl, rl, right, fr, rr)


def shifted_diff(q, base, d, axis, keep, scale):
    length = q[0].shape[axis]
    up = lambda x: pltpu.roll(x, length - 1, axis)
    flux, reach = flux_of(q, base, d, scale)
    above = between(q, flux, reach, [up(c) for c in q], [up(c) for c in flux], up(reach))
    above = [jnp.where(keep, c, 0.0) for c in above]
    return [c - pltpu.roll(c, 1, axis) for c in above]


def kernel(
    count, turn, state_in, partner_in, stencil_in, table_in, out, sides_out, lower_out, upper_out,
    state, partner, stencil, table,
    planes, mate_in, gathered, edge_out, edge_in, outer, firsts, lasts, left_in, right_in,
    plane_send, plane_recv, side_send, side_recv, load_sem,
):
    me = lax.axis_index("pass")
    blk = lax.axis_index("blk")
    odd = lax.rem(blk, 2)
    mate = blk + 1 - 2 * odd
    facing = 3 - blk
    ahead, behind = lax.rem(me + 1, count), lax.rem(me + count - 1, count)
    radial, axial, lanes = state.shape[1:]
    interface = jnp.logical_or(blk == 1, blk == 2)
    if turn is None:
        partners = list(range(count))
    else:
        sign = jnp.where(blk == 1, 1, -1)
        partners = [lax.rem(me + sign * (turn + k) + 2 * count, count) for k in range(2)]

    loads = [pltpu.make_async_copy(state_in.at[f], state.at[f], load_sem.at[f]) for f in range(5)]
    loads.append(pltpu.make_async_copy(stencil_in, stencil, load_sem.at[5]))
    loads.append(pltpu.make_async_copy(table_in, table, load_sem.at[6]))
    if turn is None:
        loads.append(pltpu.make_async_copy(partner_in, partner, load_sem.at[7]))
    for load in loads:
        load.start()

    barrier = pltpu.get_barrier_semaphore()
    for device in ((ahead, blk), (behind, blk), (me, mate)):
        pl.semaphore_signal(barrier, inc=1, device_id=device, device_id_type=MESH)

    @pl.when(interface)
    def _():
        for j in partners:
            pl.semaphore_signal(barrier, inc=1, device_id=(j, facing), device_id_type=MESH)

    for f in range(5):
        loads[f].wait()
        planes[0, f] = state[f, :, 0, :]
        planes[1, f] = state[f, :, axial - 1, :]
    plane_lane = lax.broadcasted_iota(jnp.int32, (radial, lanes), 1)

    def plane_copies():
        if turn is None:
            return [
                pltpu.make_async_remote_copy(
                    src_ref=planes.at[odd], dst_ref=gathered.at[me],
                    send_sem=plane_send.at[j], recv_sem=plane_recv.at[me],
                    device_id=(j, facing), device_id_type=MESH,
                )
                for j in partners
            ]
        pairs = [(planes.at[odd, f], gathered.at[0, f]) for f in range(5)] + [(edge_out, edge_in)]
        return [
            pltpu.make_async_remote_copy(
                src_ref=src, dst_ref=dst, send_sem=plane_send.at[k], recv_sem=plane_recv.at[k],
                device_id=(partners[k // 5], facing), device_id_type=MESH,
            )
            for k, (src, dst) in enumerate(pairs)
        ]

    def side_copy(k, src, dst, device):
        return pltpu.make_async_remote_copy(
            src_ref=src, dst_ref=dst, send_sem=side_send.at[k], recv_sem=side_recv.at[k],
            device_id=device, device_id_type=MESH,
        )

    lane = lax.broadcasted_iota(jnp.int32, (axial, lanes), 1)
    row = lax.broadcasted_iota(jnp.int32, (axial, lanes), 0)

    def pack(r, held):
        place = jnp.logical_or(lane == 2 * r, lane == lax.rem(2 * r - 1 + lanes, lanes))
        return tuple(
            jnp.where(place, pltpu.roll(state[f, r], 2 * r, 1), held[f]) for f in range(5)
        )

    held = lax.fori_loop(
        0, radial, pack, tuple(jnp.ones((axial, lanes), jnp.float32) for _ in range(5)), unroll=8
    )
    even_lane = lax.rem(lane, 2) == 0
    low_lane = lane < lanes // 2

    place = [0, 1, lanes // 2, lanes // 2 + 1, 0]

    def dense(target, cols):
        rolled = [pltpu.roll(c, p, 1) if p else c for c, p in zip(cols, place)]
        target[0] = jnp.where(
            low_lane,
            jnp.where(even_lane, rolled[0], rolled[1]),
            jnp.where(even_lane, rolled[2], rolled[3]),
        )
        target[1] = rolled[4]

    dense(firsts, held)
    dense(lasts, [pltpu.roll(c, 1, 1) for c in held])

    if turn is not None:

        @pl.when(interface)
        def _():
            edge = jnp.zeros((radial, lanes), jnp.float32)
            for f in range(5):
                first = pltpu.roll(planes[0, f], f, 1)
                last = pltpu.roll(planes[1, f], f + 1, 1)
                edge = jnp.where(plane_lane == f, jnp.where(blk == 1, last, first), edge)
            edge_out[...] = edge

    @pl.when(interface)
    def _():
        pl.semaphore_wait(barrier, 3 + len(partners))
        for copy in plane_copies():
            copy.start()

    @pl.when(jnp.logical_not(interface))
    def _():
        pl.semaphore_wait(barrier, 3)

    to_mate = side_copy(0, planes.at[1 - odd], mate_in, (me, mate))
    to_ahead = side_copy(1, lasts, left_in, (ahead, blk))
    to_behind = side_copy(2, firsts, right_in, (behind, blk))
    to_ahead.start()
    to_behind.start()
    to_mate.start()

    not_last_row = row < axial - 1
    not_last_lane = lane < lanes - 1

    def cells(r):
        return tuple(state[f, r] for f in range(5))

    def step(r, carry):
        q, base, flux, reach, below = carry
        following = cells(jnp.minimum(r + 1, radial - 1))
        base_f = basics(following)
        flux_f, reach_f = flux_of(following, base_f, 2, RADIAL_COEF)
        above = between(q, flux, reach, following, flux_f, reach_f)
        total = [c - (a - b) for c, a, b in zip(q, above, below)]
        part = shifted_diff(q, base, 1, 0, not_last_row, AXIAL_COEF)
        total = [c - a for c, a in zip(total, part)]
        part = shifted_diff(q, base, 3, 1, not_last_lane, AROUND_COEF)
        for f in range(5):
            out[f, r] = total[f] - part[f]
        return following, base_f, tuple(flux_f), reach_f, tuple(above)

    q0 = cells(0)
    base0 = basics(q0)
    flux0, reach0 = flux_of(q0, base0, 2, RADIAL_COEF)
    first = between(q0, flux0, reach0, q0, flux0, reach0)
    carry = (q0, base0, tuple(flux0), reach0, tuple(first))
    lax.fori_loop(0, radial, step, carry, unroll=4)

    def lower_faces(beside):
        for start in range(0, radial, 8):
            rows = slice(start, start + 8)
            flux = face(
                [beside[f, rows] for f in range(5)], [planes[0, f, rows] for f in range(5)], 1, AXIAL_COEF
            )
            for f in range(5):
                lower_out[f, rows] = flux[f]

    def upper_faces(beside):
        for start in range(0, radial, 8):
            rows = slice(start, start + 8)
            flux = face(
                [planes[1, f, rows] for f in range(5)], [beside[f, rows] for f in range(5)], 1, AXIAL_COEF
            )
            for f in range(5):
                upper_out[f, rows] = flux[f]

    to_mate.wait()

    @pl.when(odd == 0)
    def _():
        upper_faces(mate_in)

    @pl.when(odd == 1)
    def _():
        lower_faces(mate_in)

    to_ahead.wait()
    to_behind.wait()
    left = [
        jnp.where(even_lane, pltpu.roll(left_in[f // 4], (lanes - place[f]) % lanes, 1), held[f])
        for f in range(5)
    ]
    right = [
        jnp.where(even_lane, held[f], pltpu.roll(right_in[f // 4], lanes - 1 - place[f], 1))
        for f in range(5)
    ]
    sides = face(left, right, 3, AROUND_COEF)
    for f in range(5):
        sides_out[f] = jnp.where(even_lane, sides[f], -sides[f])

    for load in loads[5:]:
        load.wait()

    @pl.when(jnp.logical_not(interface))
    def _():
        outer[...] = planes[odd]

    @pl.when(interface)
    def _():
        if turn is None:
            for k in range(count):
                pltpu.make_async_remote_copy(
                    src_ref=planes.at[odd], dst_ref=gathered.at[k],
                    send_sem=plane_send.at[k], recv_sem=plane_recv.at[k],
                    device_id=(k, facing), device_id_type=MESH,
                ).wait()
        else:
            for copy in plane_copies():
                copy.wait()
        weights = jnp.zeros((1, lanes), jnp.float32)
        for k in range(table.shape[0]):
            weights = jnp.where(stencil[...] == k, table[k], weights)
        offset = 0 if turn is not None else lax.rem(partner[me] - me + count, count)

        def ghost(main_at, edge_at, shift, edge_lane):
            for f in range(5):
                main = gathered[0, f] if turn is not None else gathered[main_at, f]
                if turn is not None:
                    edge = pltpu.roll(edge_in[...], (edge_lane - f) % lanes, 1)
                else:
                    edge = pltpu.roll(gathered[edge_at, f], shift, 1)
                beside = jnp.where(plane_lane == edge_lane, edge, pltpu.roll(main, shift, 1))
                outer[f] = weights * main + (1.0 - weights) * beside

        @pl.when(blk == 1)
        def _():
            at = lax.rem(me + offset, count)
            ghost(at, lax.rem(at + 1, count), lanes - 1, lanes - 1)

        @pl.when(blk == 2)
        def _():
            at = lax.rem(me - offset + count, count)
            ghost(at, lax.rem(at + count - 1, count), 1, 0)

    @pl.when(odd == 0)
    def _():
        lower_faces(outer)

    @pl.when(odd == 1)
    def _():
        upper_faces(outer)


def section(turn, state, partner, stencil, weight_table):
    count = lax.axis_size("pass")
    _, radial, axial, lanes = state.shape
    hbm = pl.BlockSpec(memory_space=pltpu.HBM)
    f32 = jnp.float32
    held = count if turn is None else 1
    copies = count if turn is None else 6
    return pl.pallas_call(
        functools.partial(kernel, count, turn),
        out_shape=[
            jax.ShapeDtypeStruct(shape, f32)
            for shape in (state.shape, (5, axial, lanes), (5, radial, lanes), (5, radial, lanes))
        ],
        in_specs=[hbm] * 4,
        out_specs=[pl.BlockSpec(memory_space=pltpu.VMEM)] * 4,
        scratch_shapes=[
            pltpu.VMEM(state.shape, f32),
            pltpu.SMEM(partner.shape, jnp.int32),
            pltpu.VMEM(stencil.shape, jnp.int32),
            pltpu.SMEM(weight_table.shape, f32),
            pltpu.VMEM((2, 5, radial, lanes), f32),
            pltpu.VMEM((5, radial, lanes), f32),
            pltpu.VMEM((held, 5, radial, lanes), f32),
            pltpu.VMEM((radial, lanes), f32),
            pltpu.VMEM((radial, lanes), f32),
            pltpu.VMEM((5, radial, lanes), f32),
            pltpu.VMEM((2, axial, lanes), f32),
            pltpu.VMEM((2, axial, lanes), f32),
            pltpu.VMEM((2, axial, lanes), f32),
            pltpu.VMEM((2, axial, lanes), f32),
            pltpu.SemaphoreType.DMA((copies,)),
            pltpu.SemaphoreType.DMA((copies,)),
            pltpu.SemaphoreType.DMA((3,)),
            pltpu.SemaphoreType.DMA((3,)),
            pltpu.SemaphoreType.DMA((8,)),
        ],
        compiler_params=pltpu.CompilerParams(
            collective_id=turn or 0, has_side_effects=True, vmem_limit_bytes=24 * 1024 * 1024
        ),
        cost_estimate=pl.CostEstimate(
            flops=200 * radial * axial * lanes, bytes_accessed=8 * state.size, transcendentals=0
        ),
    )(state, partner, stencil, weight_table)


def store_kernel(value, sides, lower, upper, out, held, sem):
    _, radial, axial, lanes = value.shape
    lane = lax.broadcasted_iota(jnp.int32, (axial, lanes), 1)
    ends = jnp.logical_or(lane == 0, lane == lanes - 1)
    copies = []
    for start in range(0, radial, 8):
        rows = slice(start, start + 8)
        for f in range(5):
            for r in range(start, start + 8):
                moved = pltpu.roll(sides[f], (lanes - 2 * r) % lanes, 1) if r else sides[f]
                held[f, r] = value[f, r] + jnp.where(ends, moved, 0.0)
            held[f, rows, 0, :] = held[f, rows, 0, :] + lower[f, rows]
            held[f, rows, axial - 1, :] = held[f, rows, axial - 1, :] - upper[f, rows]
            copy = pltpu.make_async_copy(
                held.at[f, pl.ds(start, 8)], out.at[f, pl.ds(start, 8)], sem.at[start // 8, f]
            )
            copy.start()
            copies.append(copy)
    for copy in copies:
        copy.wait()


def store(value, sides, lower, upper):
    return pl.pallas_call(
        store_kernel,
        out_shape=jax.ShapeDtypeStruct(value.shape, value.dtype),
        in_specs=[pl.BlockSpec(memory_space=pltpu.VMEM)] * 4,
        out_specs=pl.BlockSpec(memory_space=pltpu.HBM),
        scratch_shapes=[
            pltpu.VMEM(value.shape, value.dtype),
            pltpu.SemaphoreType.DMA((value.shape[1] // 8, 5)),
        ],
        compiler_params=pltpu.CompilerParams(vmem_limit_bytes=24 * 1024 * 1024),
    )(value, sides, lower, upper)


def shards(state, partner, stencil, weight_table):
    count = lax.axis_size("pass")
    operands = (state, partner, stencil.reshape(1, -1), weight_table)
    if count > 8:
        return store(*section(None, *operands))
    parts = lax.switch(
        partner[0] - 1, [functools.partial(section, k) for k in range(1, count)], *operands
    )
    return store(*parts)


def solution(mesh):
    placed = (P(None, None, "blk", "pass"), P(), P("pass"), P())
    return jax.shard_map(
        shards, mesh=mesh, in_specs=placed, out_specs=P(None, None, "blk", "pass"), check_vma=False
    )
```

```python
import functools

import jax
import jax.numpy as jnp
from jax import lax
from jax.experimental import pallas as pl
from jax.experimental.pallas import tpu as pltpu
from jax.sharding import PartitionSpec as P

AXIAL_COEF = 0.4
RADIAL_COEF = 0.3
AROUND_COEF = 0.3
MESH = pl.DeviceIdType.MESH


def basics(q):
    inv = 1.0 / q[0]
    pressure = 0.4 * (q[4] - 0.5 * (q[1] * q[1] + q[2] * q[2] + q[3] * q[3]) * inv)
    square = 1.4 * pressure * inv
    return inv, pressure, square * lax.rsqrt(square)


def flux_of(q, base, d, scale):
    inv, pressure, sound = base
    u = q[d] * (inv * (0.5 * scale))
    part = pressure * (0.5 * scale)
    flux = [c * u for c in q]
    flux[d] = flux[d] + part
    flux[4] = flux[4] + pressure * u
    return flux, jnp.abs(u) + sound * (0.5 * scale)


def between(left, flux_left, reach_left, right, flux_right, reach_right):
    reach = jnp.maximum(reach_left, reach_right)
    return [
        (fl + fr) - reach * (b - a)
        for a, fl, b, fr in zip(left, flux_left, right, flux_right)
    ]


def face(left, right, d, scale):
    fl, rl = flux_of(left, basics(left), d, scale)
    fr, rr = flux_of(right, basics(right), d, scale)
    return between(left, fl, rl, right, fr, rr)


def shifted_diff(q, base, d, axis, keep, scale):
    length = q[0].shape[axis]
    up = lambda x: pltpu.roll(x, length - 1, axis)
    flux, reach = flux_of(q, base, d, scale)
    above = between(q, flux, reach, [up(c) for c in q], [up(c) for c in flux], up(reach))
    above = [jnp.where(keep, c, 0.0) for c in above]
    return [c - pltpu.roll(c, 1, axis) for c in above]


def kernel(
    count, turn, state_in, partner_in, stencil_in, table_in, out, sides_out, lower_out, upper_out,
    state, partner, stencil, table,
    planes, mate_in, gathered, edge_out, edge_in, outer, firsts, lasts, left_in, right_in,
    plane_send, plane_recv, side_send, side_recv, load_sem,
):
    me = lax.axis_index("pass")
    blk = lax.axis_index("blk")
    odd = lax.rem(blk, 2)
    mate = blk + 1 - 2 * odd
    facing = 3 - blk
    ahead, behind = lax.rem(me + 1, count), lax.rem(me + count - 1, count)
    radial, axial, lanes = state.shape[1:]
    interface = jnp.logical_or(blk == 1, blk == 2)
    if turn is None:
        partners = list(range(count))
    else:
        sign = jnp.where(blk == 1, 1, -1)
        partners = [lax.rem(me + sign * (turn + k) + 2 * count, count) for k in range(2)]

    loads = [pltpu.make_async_copy(state_in.at[f], state.at[f], load_sem.at[f]) for f in range(5)]
    loads.append(pltpu.make_async_copy(stencil_in, stencil, load_sem.at[5]))
    loads.append(pltpu.make_async_copy(table_in, table, load_sem.at[6]))
    if turn is None:
        loads.append(pltpu.make_async_copy(partner_in, partner, load_sem.at[7]))
    for load in loads:
        load.start()

    barrier = pltpu.get_barrier_semaphore()
    for device in ((ahead, blk), (behind, blk), (me, mate)):
        pl.semaphore_signal(barrier, inc=1, device_id=device, device_id_type=MESH)

    @pl.when(interface)
    def _():
        for j in partners:
            pl.semaphore_signal(barrier, inc=1, device_id=(j, facing), device_id_type=MESH)

    for f in range(5):
        loads[f].wait()
        planes[0, f] = state[f, :, 0, :]
        planes[1, f] = state[f, :, axial - 1, :]
    plane_lane = lax.broadcasted_iota(jnp.int32, (radial, lanes), 1)

    def plane_copies():
        if turn is None:
            return [
                pltpu.make_async_remote_copy(
                    src_ref=planes.at[odd], dst_ref=gathered.at[me],
                    send_sem=plane_send.at[j], recv_sem=plane_recv.at[me],
                    device_id=(j, facing), device_id_type=MESH,
                )
                for j in partners
            ]
        pairs = [(planes.at[odd, f], gathered.at[0, f]) for f in range(5)] + [(edge_out, edge_in)]
        return [
            pltpu.make_async_remote_copy(
                src_ref=src, dst_ref=dst, send_sem=plane_send.at[k], recv_sem=plane_recv.at[k],
                device_id=(partners[k // 5], facing), device_id_type=MESH,
            )
            for k, (src, dst) in enumerate(pairs)
        ]

    def side_copy(k, src, dst, device):
        return pltpu.make_async_remote_copy(
            src_ref=src, dst_ref=dst, send_sem=side_send.at[k], recv_sem=side_recv.at[k],
            device_id=device, device_id_type=MESH,
        )

    lane = lax.broadcasted_iota(jnp.int32, (axial, lanes), 1)
    row = lax.broadcasted_iota(jnp.int32, (axial, lanes), 0)

    def pack(r, held):
        place = jnp.logical_or(lane == 2 * r, lane == lax.rem(2 * r - 1 + lanes, lanes))
        return tuple(
            jnp.where(place, pltpu.roll(state[f, r], 2 * r, 1), held[f]) for f in range(5)
        )

    held = lax.fori_loop(
        0, radial, pack, tuple(jnp.ones((axial, lanes), jnp.float32) for _ in range(5)), unroll=8
    )
    even_lane = lax.rem(lane, 2) == 0
    low_lane = lane < lanes // 2

    place = [0, 1, lanes // 2, lanes // 2 + 1, 0]

    def dense(target, cols):
        rolled = [pltpu.roll(c, p, 1) if p else c for c, p in zip(cols, place)]
        target[0] = jnp.where(
            low_lane,
            jnp.where(even_lane, rolled[0], rolled[1]),
            jnp.where(even_lane, rolled[2], rolled[3]),
        )
        target[1] = rolled[4]

    dense(firsts, held)
    dense(lasts, [pltpu.roll(c, 1, 1) for c in held])

    if turn is not None:

        @pl.when(interface)
        def _():
            edge = jnp.zeros((radial, lanes), jnp.float32)
            for f in range(5):
                first = pltpu.roll(planes[0, f], f, 1)
                last = pltpu.roll(planes[1, f], f + 1, 1)
                edge = jnp.where(plane_lane == f, jnp.where(blk == 1, last, first), edge)
            edge_out[...] = edge

    @pl.when(interface)
    def _():
        pl.semaphore_wait(barrier, 3 + len(partners))
        for copy in plane_copies():
            copy.start()

    @pl.when(jnp.logical_not(interface))
    def _():
        pl.semaphore_wait(barrier, 3)

    to_mate = side_copy(0, planes.at[1 - odd], mate_in, (me, mate))
    to_ahead = side_copy(1, lasts, left_in, (ahead, blk))
    to_behind = side_copy(2, firsts, right_in, (behind, blk))
    to_ahead.start()
    to_behind.start()
    to_mate.start()

    not_last_row = row < axial - 1
    not_last_lane = lane < lanes - 1

    def cells(r):
        return tuple(state[f, r] for f in range(5))

    def step(r, carry):
        q, base, flux, reach, below = carry
        following = cells(jnp.minimum(r + 1, radial - 1))
        base_f = basics(following)
        flux_f, reach_f = flux_of(following, base_f, 2, RADIAL_COEF)
        above = between(q, flux, reach, following, flux_f, reach_f)
        total = [c - (a - b) for c, a, b in zip(q, above, below)]
        part = shifted_diff(q, base, 1, 0, not_last_row, AXIAL_COEF)
        total = [c - a for c, a in zip(total, part)]
        part = shifted_diff(q, base, 3, 1, not_last_lane, AROUND_COEF)
        for f in range(5):
            out[f, r] = total[f] - part[f]
        return following, base_f, tuple(flux_f), reach_f, tuple(above)

    q0 = cells(0)
    base0 = basics(q0)
    flux0, reach0 = flux_of(q0, base0, 2, RADIAL_COEF)
    first = between(q0, flux0, reach0, q0, flux0, reach0)
    carry = (q0, base0, tuple(flux0), reach0, tuple(first))
    lax.fori_loop(0, radial, step, carry, unroll=4)

    def lower_faces(beside):
        for start in range(0, radial, 8):
            rows = slice(start, start + 8)
            flux = face(
                [beside[f, rows] for f in range(5)], [planes[0, f, rows] for f in range(5)], 1, AXIAL_COEF
            )
            for f in range(5):
                lower_out[f, rows] = flux[f]

    def upper_faces(beside):
        for start in range(0, radial, 8):
            rows = slice(start, start + 8)
            flux = face(
                [planes[1, f, rows] for f in range(5)], [beside[f, rows] for f in range(5)], 1, AXIAL_COEF
            )
            for f in range(5):
                upper_out[f, rows] = flux[f]

    to_mate.wait_recv()

    @pl.when(odd == 0)
    def _():
        upper_faces(mate_in)

    @pl.when(odd == 1)
    def _():
        lower_faces(mate_in)

    to_ahead.wait_recv()
    to_behind.wait_recv()
    left = [
        jnp.where(even_lane, pltpu.roll(left_in[f // 4], (lanes - place[f]) % lanes, 1), held[f])
        for f in range(5)
    ]
    right = [
        jnp.where(even_lane, held[f], pltpu.roll(right_in[f // 4], lanes - 1 - place[f], 1))
        for f in range(5)
    ]
    sides = face(left, right, 3, AROUND_COEF)
    for f in range(5):
        sides_out[f] = jnp.where(even_lane, sides[f], -sides[f])

    for load in loads[5:]:
        load.wait()

    @pl.when(jnp.logical_not(interface))
    def _():
        outer[...] = planes[odd]

    @pl.when(interface)
    def _():
        if turn is None:
            for k in range(count):
                pltpu.make_async_remote_copy(
                    src_ref=planes.at[odd], dst_ref=gathered.at[k],
                    send_sem=plane_send.at[k], recv_sem=plane_recv.at[k],
                    device_id=(k, facing), device_id_type=MESH,
                ).wait_recv()
        else:
            for copy in plane_copies():
                copy.wait_recv()
        weights = jnp.zeros((1, lanes), jnp.float32)
        for k in range(table.shape[0]):
            weights = jnp.where(stencil[...] == k, table[k], weights)
        offset = 0 if turn is not None else lax.rem(partner[me] - me + count, count)

        def ghost(main_at, edge_at, shift, edge_lane):
            for f in range(5):
                main = gathered[0, f] if turn is not None else gathered[main_at, f]
                if turn is not None:
                    edge = pltpu.roll(edge_in[...], (edge_lane - f) % lanes, 1)
                else:
                    edge = pltpu.roll(gathered[edge_at, f], shift, 1)
                beside = jnp.where(plane_lane == edge_lane, edge, pltpu.roll(main, shift, 1))
                outer[f] = weights * main + (1.0 - weights) * beside

        @pl.when(blk == 1)
        def _():
            at = lax.rem(me + offset, count)
            ghost(at, lax.rem(at + 1, count), lanes - 1, lanes - 1)

        @pl.when(blk == 2)
        def _():
            at = lax.rem(me - offset + count, count)
            ghost(at, lax.rem(at + count - 1, count), 1, 0)

    @pl.when(odd == 0)
    def _():
        lower_faces(outer)

    @pl.when(odd == 1)
    def _():
        upper_faces(outer)

    for copy in (to_mate, to_ahead, to_behind):
        copy.wait_send()

    @pl.when(interface)
    def _():
        for copy in plane_copies():
            copy.wait_send()


def section(turn, state, partner, stencil, weight_table):
    count = lax.axis_size("pass")
    _, radial, axial, lanes = state.shape
    hbm = pl.BlockSpec(memory_space=pltpu.HBM)
    f32 = jnp.float32
    held = count if turn is None else 1
    copies = count if turn is None else 6
    return pl.pallas_call(
        functools.partial(kernel, count, turn),
        out_shape=[
            jax.ShapeDtypeStruct(shape, f32)
            for shape in (state.shape, (5, axial, lanes), (5, radial, lanes), (5, radial, lanes))
        ],
        in_specs=[hbm] * 4,
        out_specs=[pl.BlockSpec(memory_space=pltpu.VMEM)] * 4,
        scratch_shapes=[
            pltpu.VMEM(state.shape, f32),
            pltpu.SMEM(partner.shape, jnp.int32),
            pltpu.VMEM(stencil.shape, jnp.int32),
            pltpu.SMEM(weight_table.shape, f32),
            pltpu.VMEM((2, 5, radial, lanes), f32),
            pltpu.VMEM((5, radial, lanes), f32),
            pltpu.VMEM((held, 5, radial, lanes), f32),
            pltpu.VMEM((radial, lanes), f32),
            pltpu.VMEM((radial, lanes), f32),
            pltpu.VMEM((5, radial, lanes), f32),
            pltpu.VMEM((2, axial, lanes), f32),
            pltpu.VMEM((2, axial, lanes), f32),
            pltpu.VMEM((2, axial, lanes), f32),
            pltpu.VMEM((2, axial, lanes), f32),
            pltpu.SemaphoreType.DMA((copies,)),
            pltpu.SemaphoreType.DMA((copies,)),
            pltpu.SemaphoreType.DMA((3,)),
            pltpu.SemaphoreType.DMA((3,)),
            pltpu.SemaphoreType.DMA((8,)),
        ],
        compiler_params=pltpu.CompilerParams(
            collective_id=turn or 0, has_side_effects=True, vmem_limit_bytes=24 * 1024 * 1024
        ),
        cost_estimate=pl.CostEstimate(
            flops=200 * radial * axial * lanes, bytes_accessed=8 * state.size, transcendentals=0
        ),
    )(state, partner, stencil, weight_table)


def store_kernel(value, sides, lower, upper, out, held, sem):
    _, radial, axial, lanes = value.shape
    lane = lax.broadcasted_iota(jnp.int32, (axial, lanes), 1)
    ends = jnp.logical_or(lane == 0, lane == lanes - 1)
    copies = []
    for start in range(0, radial, 8):
        rows = slice(start, start + 8)
        for f in range(5):
            for r in range(start, start + 8):
                moved = pltpu.roll(sides[f], (lanes - 2 * r) % lanes, 1) if r else sides[f]
                held[f, r] = value[f, r] + jnp.where(ends, moved, 0.0)
            held[f, rows, 0, :] = held[f, rows, 0, :] + lower[f, rows]
            held[f, rows, axial - 1, :] = held[f, rows, axial - 1, :] - upper[f, rows]
            copy = pltpu.make_async_copy(
                held.at[f, pl.ds(start, 8)], out.at[f, pl.ds(start, 8)], sem.at[start // 8, f]
            )
            copy.start()
            copies.append(copy)
    for copy in copies:
        copy.wait()


def store(value, sides, lower, upper):
    return pl.pallas_call(
        store_kernel,
        out_shape=jax.ShapeDtypeStruct(value.shape, value.dtype),
        in_specs=[pl.BlockSpec(memory_space=pltpu.VMEM)] * 4,
        out_specs=pl.BlockSpec(memory_space=pltpu.HBM),
        scratch_shapes=[
            pltpu.VMEM(value.shape, value.dtype),
            pltpu.SemaphoreType.DMA((value.shape[1] // 8, 5)),
        ],
        compiler_params=pltpu.CompilerParams(vmem_limit_bytes=24 * 1024 * 1024),
    )(value, sides, lower, upper)


def shards(state, partner, stencil, weight_table):
    count = lax.axis_size("pass")
    operands = (state, partner, stencil.reshape(1, -1), weight_table)
    if count > 8:
        return store(*section(None, *operands))
    parts = lax.switch(
        partner[0] - 1, [functools.partial(section, k) for k in range(1, count)], *operands
    )
    return store(*parts)


def solution(mesh):
    placed = (P(None, None, "blk", "pass"), P(), P("pass"), P())
    return jax.shard_map(
        shards, mesh=mesh, in_specs=placed, out_specs=P(None, None, "blk", "pass"), check_vma=False
    )
```
